256 devices in a mesh: dp: 32 (over y, z_lo, core), tensor: 8 (over z_hi, x).
Axes of the slice: x: 4, y: 4, z: 8 (z_hi: 2, z_lo: 4; z = z_hi * 4 + z_lo), core: 2. Of those that a mesh axis runs over, the one named last changes fastest.
Arguments:
- input_rows: bfloat16 [16384, 16384], P('dp', 'tensor'), may hold values from -6 to 6
- frozen_projection_output: bfloat16 [16384, 18432], P('dp', 'tensor'), may hold values from -100 to 100
- output_gradient: bfloat16 [16384, 16384], P('dp', 'tensor'), may hold values from -0.29882812 to 0.29882812
- segments: int32 [32, 512], P('dp'), may hold values from 0 to 7, never falling along the last dimension, each value on 1 to 128 neighbouring positions
- adapter_of_group: int32 [32, 1], replicated, may hold values from 0 to 7
- adapter_down_weight: bfloat16 [8, 48, 16384], P(None, None, 'tensor'), may hold values from -0.21875 to 0.21875
- adapter_up_weight: bfloat16 [8, 16, 18432], P(None, None, 'tensor'), may hold values from -0.19921875 to 0.19921875
Outputs:
- grad_down: float32 [8, 48, 16384], P(None, None, 'tensor')
- grad_up: float32 [8, 16, 18432], P(None, None, 'tensor')
The draws below stay inside these ranges and needn't reach their ends.
Inputs may be any that keep to these rules, and one draw needn't show every extreme that they name: `segments`: ids never fall along a group's tokens; a document holds at most 128 tokens. `adapter_of_group`: every adapter is trained by at least one data group.
All inputs are finite; a program needn't handle non-finite values.
Results may differ from the reference program's by a relative error of at most 0.03.
Values may be sent and summed in bfloat16 or wider, within the bound.
A program may use at most 128 MiB of HBM per device.

```python
import math
import jax
import jax.numpy as jnp
import numpy as np
from jax import lax

MODEL_WIDTH = 16384
HQ = 128
KEY_HEADS = 8
HEAD_SIZE = 128
ADAPTER_RANK = 16
ADAPTER_NUMBER = 8
SEQ = 512
QUERY_PER_KEY = 16
PROJECTION_COLS = 18432
GROUPS = 32
TOKEN_TOTAL = 16384
N_TENSOR = 8


def draw_input_rows(key, part):
    key = jax.random.fold_in(key, 11)
    full_shape = (TOKEN_TOTAL, MODEL_WIDTH)
    value_matrix = jnp.clip(jax.random.normal(key, full_shape, jnp.float32), -6.0, 6.0)
    return value_matrix.astype(jnp.bfloat16)


def draw_frozen_projection_output(key, part):
    key = jax.random.fold_in(key, 23)
    column_roles = QUERY_PER_KEY + 2
    value_matrix = jnp.clip(jax.random.normal(key, (TOKEN_TOTAL, KEY_HEADS, column_roles, HEAD_SIZE), jnp.float32), -6.0, 6.0)
    return value_matrix.reshape(TOKEN_TOTAL, KEY_HEADS * column_roles * HEAD_SIZE).astype(jnp.bfloat16)


def steps_of(stream_key, extent, shards, least, top_value):
    def one(dim, parts):
        draws = jax.random.uniform(jax.random.fold_in(jax.random.fold_in(stream_key, 6), dim), (parts,), jnp.float32, least / len(shards), top_value / len(shards))
        return jnp.repeat(jnp.exp(draws), extent[dim] // parts).reshape((-1,) + (1,) * (len(extent) - dim - 1))

    level = one(*shards[0])
    for cut in shards[1:]:
        level = level * one(*cut)
    return level


def choose_distinct(own_key, rows, amount, top, lift):
    ranking = jax.random.permutation(jax.random.fold_in(own_key, 1), amount)
    boost = ranking
    for power in range(3):
        boost = boost * boost // amount
    boost = boost * lift // amount
    tickets = jax.random.randint(jax.random.fold_in(own_key, 2), (rows, amount), 0, 4096) + boost
    sure = jax.random.permutation(jax.random.fold_in(own_key, 3), rows)[jnp.arange(amount) % rows]
    tickets = jnp.where(jnp.arange(rows)[:, None] == sure[None, :], 1 << 14, tickets)
    priority = tickets * amount + jnp.arange(amount)
    return lax.top_k(priority.astype(jnp.int32), top)[1].astype(jnp.int32)


def split_up(number_of, total, limit, slope):
    loads = [(1 << 20) // math.isqrt(standing ** slope) + 1 for standing in range(2, number_of + 1)]
    spare, holding = total - limit - (number_of - 1), [1] * (number_of - 1)
    while spare > 0:
        free = [i for i in range(number_of - 1) if holding[i] < limit]
        mass, left = sum([loads[i] for i in free]), spare
        for i in free:
            extra = min(limit - holding[i], max(1, left * loads[i] // mass), spare)
            holding[i] = holding[i] + extra
            spare = spare - extra
    return np.array([limit] + holding)


def ragged_sizes(key, amount, total, limit, lean):
    if amount == 2:
        one = jax.random.randint(key, (), max(1, total - limit), min(limit, total - 1) + 1)
        return jnp.stack([one, total - one])
    tallies = jnp.asarray(split_up(amount, total, limit, lean), jnp.int32)
    couples = (amount - 1) // 2
    donor, taker = tallies[1:1 + 2 * couples:2], tallies[2:2 + 2 * couples:2]
    margin = jnp.minimum(donor - 1, limit - taker)
    shifted = jax.random.randint(jax.random.fold_in(key, 1), (couples,), 0, 1 << 20) % (margin + 1)
    tallies = tallies.at[1:1 + 2 * couples:2].set(donor - shifted).at[2:2 + 2 * couples:2].set(taker + shifted)
    return tallies[jax.random.permutation(jax.random.fold_in(key, 2), amount)]


def noise(rng, shape, spread, most, cuts=(), held_as=jnp.bfloat16):
    gain = steps_of(rng, shape, cuts, -0.22, 0.18) if cuts else 1.0
    array = jax.random.normal(rng, shape, jnp.float32) * spread * gain
    return jnp.minimum(jnp.maximum(array, -most), most).astype(held_as)


def setup_inputs(seed: int = 0) -> dict:
    keys = jax.random.split(jax.random.key(seed), 8)
    input_rows = draw_input_rows(jax.random.fold_in(keys[7], 71), 0)
    frozen_projection_output = draw_frozen_projection_output(jax.random.fold_in(keys[7], 71), 0)
    output_gradient = noise(keys[2], (TOKEN_TOTAL, HQ * HEAD_SIZE), 0.05, 0.29882812, ((0, 32), (1, 8)))
    segments = jax.vmap(lambda own: jnp.searchsorted(jnp.cumsum(ragged_sizes(own, 8, SEQ, SEQ // 4, 1)), jnp.arange(SEQ), side="right"))(jax.random.split(keys[3], GROUPS)).reshape((GROUPS, SEQ)).astype(jnp.int32)
    adapter_of_group = choose_distinct(keys[4], GROUPS, ADAPTER_NUMBER, 1, 2048)
    adapter_down_weight = noise(keys[5], (ADAPTER_NUMBER, 3 * ADAPTER_RANK, MODEL_WIDTH), (MODEL_WIDTH // 20) ** -0.5, 0.21875, ((2, 8),))
    adapter_up_weight = noise(keys[6], (ADAPTER_NUMBER, ADAPTER_RANK, PROJECTION_COLS), 0.034, 0.19921875, ((2, 8),))
    return {"input_rows": input_rows, "frozen_projection_output": frozen_projection_output, "output_gradient": output_gradient, "segments": segments, "adapter_of_group": adapter_of_group, "adapter_down_weight": adapter_down_weight, "adapter_up_weight": adapter_up_weight}


adapter_scale = 0.5
masked_score = -1e30


def saved_values(value):
    return lax.optimization_barrier(value.astype(jnp.bfloat16))


def broadened(value):
    return value.astype(jnp.float32)


def attend(query_rows, grad_rows, key_rows, value_rows, allowed):
    head_count = query_rows.shape[0]
    sequence_length = key_rows.shape[0]
    block_heads = 4 if head_count % 4 == 0 else head_count
    scaling = key_rows.shape[-1] ** -0.5
    keys_wide = broadened(key_rows)
    values_wide = broadened(value_rows)

    def block_step(totals, inputs):
        queries, head_gradients = inputs
        queries_wide = broadened(queries)
        grads_wide = broadened(head_gradients)
        scores = jnp.einsum('hqd,kd->hqk', queries_wide, keys_wide) * scaling
        scores = jnp.where(allowed[None], scores, masked_score)
        row_max = jnp.max(scores, axis=-1, keepdims=True)
        weights = jnp.exp(scores - row_max)
        probs = weights / jnp.sum(weights, axis=-1, keepdims=True)
        probs_low = broadened(saved_values(probs))
        value_gradient = totals[1] + jnp.einsum('hqk,hqd->kd', probs_low, grads_wide)
        prob_grad = jnp.einsum('hqd,kd->hqk', grads_wide, values_wide)
        row_dot = jnp.sum(probs * prob_grad, axis=-1, keepdims=True)
        score_grad = broadened(saved_values(probs * (prob_grad - row_dot) * scaling))
        query_gradient = jnp.einsum('hqk,kd->hqd', score_grad, keys_wide)
        key_gradient = totals[0] + jnp.einsum('hqk,hqd->kd', score_grad, queries_wide)
        return (key_gradient, value_gradient), query_gradient

    zeros_kv = jnp.zeros(key_rows.shape, jnp.float32)
    stacked = (query_rows.reshape(head_count // block_heads, block_heads, sequence_length, -1),
               grad_rows.reshape(head_count // block_heads, block_heads, sequence_length, -1))
    (key_gradient, value_gradient), query_gradient = lax.scan(block_step, (zeros_kv, zeros_kv), stacked)
    return query_gradient.reshape(head_count, sequence_length, -1), key_gradient, value_gradient


def group_terms(x_group, frozen_group_rows, group_gradient, seg_ids, down_mapping, up_mapping):
    sequence_length = x_group.shape[0]
    slice_width = MODEL_WIDTH // N_TENSOR
    down_sliced = broadened(down_mapping).reshape(3 * ADAPTER_RANK, N_TENSOR, slice_width)
    rows_sliced = broadened(x_group).reshape(sequence_length, N_TENSOR, slice_width)
    slice_terms = jnp.einsum('rnw,snw->nrs', down_sliced, rows_sliced, precision=lax.Precision.HIGHEST)
    low_rank = saved_values(jnp.sum(broadened(saved_values(slice_terms)), axis=0))
    low_wide = broadened(low_rank)
    frozen_columns = frozen_group_rows.reshape(sequence_length, KEY_HEADS, QUERY_PER_KEY + 2, HEAD_SIZE)
    upward_columns = broadened(up_mapping).reshape(ADAPTER_RANK, KEY_HEADS, QUERY_PER_KEY + 2, HEAD_SIZE)
    reduced_query = low_wide[:ADAPTER_RANK]
    reduced_key = low_wide[ADAPTER_RANK:2 * ADAPTER_RANK]
    reduced_value = low_wide[2 * ADAPTER_RANK:]
    full_queries = saved_values(broadened(frozen_columns[:, :, :QUERY_PER_KEY]) + adapter_scale * jnp.einsum('oc,oqum->cqum', reduced_query, upward_columns[:, :, :QUERY_PER_KEY]))
    full_keys = saved_values(broadened(frozen_columns[:, :, QUERY_PER_KEY]) + adapter_scale * jnp.einsum('qv,qaj->vaj', reduced_key, upward_columns[:, :, QUERY_PER_KEY]))
    full_values = saved_values(broadened(frozen_columns[:, :, QUERY_PER_KEY + 1]) + adapter_scale * jnp.einsum('qv,qaj->vaj', reduced_value, upward_columns[:, :, QUERY_PER_KEY + 1]))
    position = jnp.arange(sequence_length)
    allowed = (position[:, None] >= position[None, :]) & (seg_ids[:, None] == seg_ids[None, :])
    head_gradients = group_gradient.reshape(sequence_length, KEY_HEADS, QUERY_PER_KEY, HEAD_SIZE)

    def per_head(inputs):
        queries, grads_here, key_rows, value_rows = inputs
        return attend(queries, grads_here, key_rows, value_rows, allowed)

    query_gradient, key_gradient, value_gradient = lax.map(per_head, (
        jnp.transpose(full_queries, (1, 2, 0, 3)), jnp.transpose(head_gradients, (1, 2, 0, 3)),
        jnp.transpose(full_keys, (1, 0, 2)), jnp.transpose(full_values, (1, 0, 2))))
    query_gradient = broadened(saved_values(query_gradient))
    key_gradient = broadened(saved_values(key_gradient))
    value_gradient = broadened(saved_values(value_gradient))
    query_up_weight = adapter_scale * jnp.einsum('py,fiym->pfim', reduced_query, query_gradient)
    key_up_weight = adapter_scale * jnp.einsum('io,hoy->ihy', reduced_key, key_gradient)
    value_up_weight = adapter_scale * jnp.einsum('io,hoy->ihy', reduced_value, value_gradient)
    up_grad = jnp.concatenate([query_up_weight, key_up_weight[:, :, None], value_up_weight[:, :, None]], axis=2).reshape(ADAPTER_RANK, -1)
    head_query_gradient = adapter_scale * jnp.einsum('noxe,oxwe->onw', upward_columns[:, :, :QUERY_PER_KEY], query_gradient)
    head_key_gradient = adapter_scale * jnp.einsum('qjl,jnl->jqn', upward_columns[:, :, QUERY_PER_KEY], key_gradient)
    head_value_gradient = adapter_scale * jnp.einsum('qjl,jnl->jqn', upward_columns[:, :, QUERY_PER_KEY + 1], value_gradient)
    head_terms = jnp.concatenate([head_query_gradient, head_key_gradient, head_value_gradient], axis=1)
    slice_sums = jnp.sum(head_terms.reshape(N_TENSOR, KEY_HEADS // N_TENSOR, 3 * ADAPTER_RANK, sequence_length), axis=1)
    low_grad = saved_values(jnp.sum(broadened(saved_values(slice_sums)), axis=0))
    down_grad = jnp.dot(low_grad, x_group, preferred_element_type=jnp.float32)
    return down_grad, up_grad


def reference(input_rows, frozen_projection_output, output_gradient, segments, adapter_of_group, adapter_down_weight, adapter_up_weight):
    adapter_ids = adapter_of_group[:, 0]
    number_adapters = adapter_down_weight.shape[0]

    def per_group(totals, inputs):
        x_group, frozen_group_rows, group_gradient, seg_ids, matching_adapter = inputs
        down_grad, up_grad = group_terms(x_group, frozen_group_rows, group_gradient, seg_ids,
                                         adapter_down_weight[matching_adapter], adapter_up_weight[matching_adapter])
        owner = (jnp.arange(number_adapters) == matching_adapter).astype(jnp.float32)
        return (totals[0] + owner[:, None, None] * down_grad[None],
                totals[1] + owner[:, None, None] * up_grad[None]), None

    blank_array = (jnp.zeros(adapter_down_weight.shape, jnp.float32), jnp.zeros(adapter_up_weight.shape, jnp.float32))
    inputs = (input_rows.reshape(GROUPS, SEQ, MODEL_WIDTH), frozen_projection_output.reshape(GROUPS, SEQ, PROJECTION_COLS),
              output_gradient.reshape(GROUPS, SEQ, HQ * HEAD_SIZE), segments, adapter_ids)
    (grad_down, grad_up), unused = lax.scan(per_group, blank_array, inputs)
    return grad_down, grad_up
```

```python
import functools
import math

import jax
import jax.numpy as jnp
from jax import lax
from jax.experimental import pallas as pl
from jax.experimental.pallas import tpu as pltpu
from jax.sharding import PartitionSpec as P

MESH = pl.DeviceIdType.MESH
VMEM = pltpu.VMEM
SMEM = pltpu.SMEM
DMA = pltpu.SemaphoreType.DMA

HEAD = 128
RANK = 16
HEADS = 16
KINDS = 3
BLOCK = 128
N_TENSOR = 8
N_X = 4
N_Y = 4
N_Z = 4
CHIPS = N_Y * N_Z
MEMBERS = 2 * CHIPS
ADAPTERS = 8
STEP_HEADS = 4
masked_score = -1e30

NT = (((1,), (1,)), ((), ()))
TN = (((0,), (0,)), ((), ()))
NN = (((1,), (0,)), ((), ()))


def matmul(a, b, dims=NN):
    return lax.dot_general(a, b, dims, preferred_element_type=jnp.float32)


def vmem():
    return pl.BlockSpec(memory_space=VMEM)


def smem():
    return pl.BlockSpec(memory_space=SMEM)


def greet_tensor(barrier):
    dp, me = lax.axis_index("dp"), lax.axis_index("tensor")
    for d in range(1, N_TENSOR):
        other = (me + d) % N_TENSOR
        pl.semaphore_signal(barrier, inc=1, device_id=(dp, other), device_id_type=MESH)


def tensor_scatter(part, inbox, send, recv):
    dp, me = lax.axis_index("dp"), lax.axis_index("tensor")
    copies = []
    for d in range(1, N_TENSOR):
        other = (me + d) % N_TENSOR
        copies.append(
            pltpu.make_async_remote_copy(
                src_ref=part.at[other % N_X],
                dst_ref=inbox.at[me],
                send_sem=send.at[d - 1],
                recv_sem=recv.at[d - 1],
                device_id=(dp, other),
                device_id_type=MESH,
            )
        )
        copies[-1].start()
    inbox[me] = part[me % N_X]
    return copies


def tensor_reduce(inbox, full):
    me = lax.axis_index("tensor")
    total = inbox[0].astype(jnp.float32)
    for i in range(1, N_TENSOR):
        total = total + inbox[i].astype(jnp.float32)
    full[me % N_X] = total.astype(jnp.bfloat16)


def tensor_gather(full, send, recv):
    dp, me = lax.axis_index("dp"), lax.axis_index("tensor")
    x, high = me % N_X, me // N_X
    copies = []
    for d in range(1, N_X):
        other = high * N_X + (x + d) % N_X
        copies.append(
            pltpu.make_async_remote_copy(
                src_ref=full.at[x],
                dst_ref=full.at[x],
                send_sem=send.at[d - 1],
                recv_sem=recv.at[d - 1],
                device_id=(dp, other),
                device_id_type=MESH,
            )
        )
        copies[-1].start()
    return copies


def wait_all(copies):
    for copy in copies:
        copy.wait()


def project_kernel(ids, x_ref, down_ref, low_ref, part, inbox, full, s1, r1, s2, r2):
    barrier = pltpu.get_barrier_semaphore()
    greet_tensor(barrier)
    adapter = ids[lax.axis_index("dp"), 0]
    down = down_ref[adapter]
    low = matmul(down, x_ref[...], NT)
    for b in range(N_X):
        part[b] = low[:, b * BLOCK : (b + 1) * BLOCK].astype(jnp.bfloat16)
    pl.semaphore_wait(barrier, N_TENSOR - 1)
    wait_all(tensor_scatter(part, inbox, s1, r1))
    tensor_reduce(inbox, full)
    wait_all(tensor_gather(full, s2, r2))
    low_ref[...] = full[...]


def attention_kernel(
    ids, base_ref, grad_ref, seg_ref, low_ref, up_ref, plow_ref, upout_ref,
    kwin, vwin, ktrans, bias, qs, gs, dk_acc, dv_acc, gup_q, plow_q, up_half,
):
    i = pl.program_id(0)
    adapter = ids[lax.axis_index("dp"), 0]
    kcols = pl.ds(HEADS * HEAD, HEAD)
    vcols = pl.ds((HEADS + 1) * HEAD, HEAD)
    scale = 1.0 / math.sqrt(HEAD)

    @pl.when(i == 0)
    def _():
        up_half[...] = (up_ref[adapter].astype(jnp.float32) * 0.5).astype(jnp.bfloat16)
        kwin[BLOCK:] = jnp.zeros((BLOCK, HEAD), jnp.bfloat16)
        vwin[BLOCK:] = jnp.zeros((BLOCK, HEAD), jnp.bfloat16)
        dk_acc[...] = jnp.zeros_like(dk_acc)
        dv_acc[...] = jnp.zeros_like(dv_acc)
        gup_q[...] = jnp.zeros_like(gup_q)

    low_q = low_ref[i, 0:RANK]
    low_k = low_ref[i, RANK : 2 * RANK]
    low_v = low_ref[i, 2 * RANK :]

    kwin[:BLOCK] = kwin[BLOCK:]
    vwin[:BLOCK] = vwin[BLOCK:]
    key = base_ref[:, kcols].astype(jnp.float32) + matmul(low_k, up_half[:, kcols], TN)
    value = base_ref[:, vcols].astype(jnp.float32) + matmul(low_v, up_half[:, vcols], TN)
    kwin[BLOCK:] = key.astype(jnp.bfloat16)
    vwin[BLOCK:] = value.astype(jnp.bfloat16)
    ktrans[...] = kwin[...].astype(jnp.float32).T.astype(jnp.bfloat16)

    now = seg_ref[0, pl.ds(pl.multiple_of(i * BLOCK, BLOCK), BLOCK)]
    before = seg_ref[0, pl.ds(pl.multiple_of(jnp.maximum(i - 1, 0) * BLOCK, BLOCK), BLOCK)]
    here = jnp.broadcast_to(now.astype(jnp.float32)[None, :], (BLOCK, BLOCK))
    old = jnp.broadcast_to(before.astype(jnp.float32)[None, :], (BLOCK, BLOCK))
    old = jnp.where(i == 0, -1.0, old)
    u = lax.broadcasted_iota(jnp.int32, (BLOCK, BLOCK), 0)
    t = lax.broadcasted_iota(jnp.int32, (BLOCK, BLOCK), 1)
    bias[:BLOCK] = jnp.where(old.T == here, 0.0, masked_score)
    bias[BLOCK:] = jnp.where((here.T == here) & (u <= t), 0.0, masked_score)

    plow_q[...] = jnp.zeros_like(plow_q)
    wide = STEP_HEADS * HEAD

    def heads_step(s, carry):
        cols = pl.ds(pl.multiple_of(s * wide, wide), wide)
        up_here = up_half[:, cols]
        q_wide = base_ref[:, cols].astype(jnp.float32) + matmul(low_q, up_here, TN)
        q_wide = q_wide.astype(jnp.bfloat16)
        g_wide = grad_ref[:, cols]
        for h in range(STEP_HEADS):
            qs[h * BLOCK : (h + 1) * BLOCK] = q_wide[:, h * HEAD : (h + 1) * HEAD]
            gs[h * BLOCK : (h + 1) * BLOCK] = g_wide[:, h * HEAD : (h + 1) * HEAD]
        q, g = qs[...], gs[...]
        mask = jnp.concatenate([bias[...]] * STEP_HEADS, axis=1)
        scores = matmul(kwin[...], q, NT) * (scale * math.log2(math.e)) + mask
        top = jnp.max(scores, axis=0, keepdims=True)
        weights = jnp.exp2(scores - top)
        total = jnp.sum(weights, axis=0, keepdims=True)
        probs = weights * (1.0 / total)
        prob_grad = matmul(vwin[...], g, NT)
        row_dot = jnp.sum(probs * prob_grad, axis=0, keepdims=True)
        score_grad = (probs * (prob_grad - row_dot)).astype(jnp.bfloat16)
        rows = pl.ds(pl.multiple_of(i * BLOCK, BLOCK), 2 * BLOCK)
        dv_acc[rows] += matmul(probs.astype(jnp.bfloat16), g)
        dk_acc[rows] += matmul(score_grad, q)
        dq = (matmul(ktrans[...], score_grad) * scale).astype(jnp.bfloat16)
        dq = jnp.concatenate(
            [dq[:, h * BLOCK : (h + 1) * BLOCK] for h in range(STEP_HEADS)], axis=0
        )
        plow_q[...] += matmul(up_here, dq)
        gup_q[:, cols] += matmul(low_q, dq, NT)
        return carry

    lax.fori_loop(0, HEADS // STEP_HEADS, heads_step, 0)
    plow_ref[i, 0:RANK] = plow_q[...].astype(jnp.bfloat16)

    @pl.when(i == pl.num_programs(0) - 1)
    def _():
        dk = (dk_acc[BLOCK:] * scale).astype(jnp.bfloat16)
        dv = dv_acc[BLOCK:].astype(jnp.bfloat16)
        part_k = matmul(up_half[:, kcols], dk, NT)
        part_v = matmul(up_half[:, vcols], dv, NT)
        gup_k = jnp.zeros((RANK, HEAD), jnp.float32)
        gup_v = jnp.zeros((RANK, HEAD), jnp.float32)
        for b in range(4):
            own = slice(b * BLOCK, (b + 1) * BLOCK)
            plow_ref[b, RANK : 2 * RANK] = part_k[:, own].astype(jnp.bfloat16)
            plow_ref[b, 2 * RANK :] = part_v[:, own].astype(jnp.bfloat16)
            gup_k += matmul(low_ref[b, RANK : 2 * RANK], dk[own])
            gup_v += matmul(low_ref[b, 2 * RANK :], dv[own])
        gup_k, gup_v = gup_k * 0.5, gup_v * 0.5
        for j in range(CHIPS):
            upout_ref[j, 0:RANK] = (gup_q[:, j * HEAD : (j + 1) * HEAD] * 0.5).astype(jnp.bfloat16)
            mine = (adapter == j // 2).astype(jnp.float32)
            upout_ref[j, RANK:] = ((gup_v if j % 2 else gup_k) * mine).astype(jnp.bfloat16)


def split_dp():
    dp = lax.axis_index("dp")
    return dp // 2, dp % 2


def scatter(src, inbox, core_to, send, recv):
    dp, tensor = lax.axis_index("dp"), lax.axis_index("tensor")
    chip, core = split_dp()

    def one(k, carry):
        p = (chip + k) % CHIPS
        pltpu.make_async_remote_copy(
            src_ref=src.at[p],
            dst_ref=inbox.at[dp],
            send_sem=send.at[k],
            recv_sem=recv,
            device_id=(2 * p + core_to, tensor),
            device_id_type=MESH,
        ).start()
        return carry

    lax.fori_loop(1, CHIPS, one, 0)

    @pl.when(core == core_to)
    def _():
        pltpu.make_async_copy(src.at[chip], inbox.at[dp], recv).start()

    @pl.when(core != core_to)
    def _():
        one(0, 0)


def scatter_sent(src, inbox, core_to, send, recv):
    dp, tensor = lax.axis_index("dp"), lax.axis_index("tensor")
    chip, core = split_dp()

    def one(k, carry):
        pltpu.make_async_remote_copy(
            src_ref=src.at[chip],
            dst_ref=inbox.at[dp],
            send_sem=send.at[k],
            recv_sem=recv,
            device_id=(2 * chip + core_to, tensor),
            device_id_type=MESH,
        ).wait_send()
        return carry

    lax.fori_loop(1, CHIPS, one, 0)

    @pl.when(core != core_to)
    def _():
        one(0, 0)


def arrived(whole, sem):
    pltpu.make_async_copy(whole, whole, sem).wait()


def sum_adapters(ids, inbox, rows, out, slot):
    def one(m, sums):
        term = inbox[m, rows].astype(jnp.float32)
        adapter = ids[m, 0]
        return tuple(
            sums[a] + term * (adapter == a).astype(jnp.float32) for a in range(ADAPTERS)
        )

    zero = jnp.zeros((rows.stop - rows.start, HEAD), jnp.float32)
    sums = lax.fori_loop(0, MEMBERS, one, (zero,) * ADAPTERS)
    for a in range(ADAPTERS):
        out[slot, a] = sums[a].astype(jnp.bfloat16)


class Stream:
    def __init__(self, out, owner, sems):
        self.out, self.owner = out, owner
        self.zs, self.zr, self.ys, self.yr, self.fs, self.fr, self.cs, self.cr = sems
        self.half = out.shape[1] // 2
        self.tensor = lax.axis_index("tensor")
        self.chip, self.core = split_dp()
        self.y, self.z = self.chip // N_Z, self.chip % N_Z

    def copy(self, slot, chip_to, core_to, send, recv, part=None):
        ref = self.out.at[slot] if part is None else self.out.at[slot, part]
        return pltpu.make_async_remote_copy(
            src_ref=ref,
            dst_ref=ref,
            send_sem=send,
            recv_sem=recv,
            device_id=(2 * chip_to + core_to, self.tensor),
            device_id_type=MESH,
        )

    def at(self, y, z):
        return (y % N_Y) * N_Z + z % N_Z

    def z_copy(self, d):
        return self.copy(
            self.chip, self.at(self.y, self.z + d), self.owner, self.zs.at[d - 1], self.zr.at[d - 1]
        )

    def y_copy(self, dz, side):
        to = self.at(self.y + (1 if side == 0 else 3), self.z)
        slot = self.at(self.y, self.z + N_Z - dz)
        n = 2 * dz + side
        return self.copy(slot, to, self.owner, self.ys.at[n], self.yr.at[n])

    def y_arrival(self, dz, side):
        n = 2 * dz + side
        return self.copy(
            self.y_slot(dz, side), self.chip, self.owner, self.ys.at[n], self.yr.at[n]
        )

    def y_slot(self, dz, side):
        return self.at(self.y + (3 if side == 0 else 1), self.z + N_Z - dz)

    def part(self, side):
        n = self.out.shape[1]
        return pl.ds(0, self.half) if side == 0 else pl.ds(self.half, n - self.half)

    def forward(self, dz, side):
        to = self.at(self.y + (1 if side == 0 else 3), self.z)
        slot = self.y_slot(dz, side)
        n = 2 * dz + side
        return self.copy(slot, to, self.owner, self.fs.at[n], self.fr.at[n], self.part(side))

    def forwarded(self, dz, side):
        slot = self.at(self.y + 2, self.z + N_Z - dz)
        n = 2 * dz + side
        return self.copy(slot, self.chip, self.owner, self.fs.at[n], self.fr.at[n], self.part(side))

    def twin(self, n, slot):
        return self.copy(slot, self.chip, 1 - self.owner, self.cs.at[n], self.cr)

    def start(self):
        for d in (1, 3, 2):
            self.z_copy(d).start()
        for side in range(2):
            self.y_copy(0, side).start()
        self.twin(0, self.chip).start()

    def spread(self):
        for dz in (1, 3, 2):
            self.z_copy(dz).wait_recv()
            for side in range(2):
                self.y_copy(dz, side).start()
            self.twin(dz, self.at(self.y, self.z + N_Z - dz)).start()

    def pass_on(self):
        for dz in (0, 1, 3, 2):
            for side in range(2):
                self.y_arrival(dz, side).wait_recv()
                self.forward(dz, side).start()
                self.twin(4 + 2 * dz + side, self.y_slot(dz, side)).start()

    def finish(self):
        for dz in (0, 1, 3, 2):
            for side in range(2):
                self.forwarded(dz, side).wait_recv()
            self.twin(12 + dz, self.at(self.y + 2, self.z + N_Z - dz)).start()
        for d in range(1, N_Z):
            self.z_copy(d).wait_send()
        for dz in range(N_Z):
            for side in range(2):
                self.y_copy(dz, side).wait_send()
                self.forward(dz, side).wait_send()
        for n in range(CHIPS):
            self.twin(n, self.chip).wait_send()

    def receive(self):
        arrived(self.out, self.cr)


STREAM_SEMS = [DMA((3,)), DMA((3,))] + [DMA((8,))] * 4 + [DMA((CHIPS,)), DMA]


def adapters_kernel(
    ids, x_ref, plow_ref, up_part, out_a, out_b, out_u,
    inbox, full, s1, r1, s2, r2,
    down_a, down_b, in_a, in_b, in_u, sa, sb, su, ra, rb, ru, *sems,
):
    chip, core = split_dp()
    tensor, dp = lax.axis_index("tensor"), lax.axis_index("dp")
    barrier = pltpu.get_barrier_semaphore()
    greet_tensor(barrier)

    def greet(k, carry):
        other = (dp + k) % MEMBERS
        pl.semaphore_signal(barrier, inc=1, device_id=(other, tensor), device_id_type=MESH)
        return carry

    lax.fori_loop(1, MEMBERS, greet, 0)
    pl.semaphore_wait(barrier, N_TENSOR - 1 + MEMBERS - 1)

    stream_a = Stream(out_a, 0, sems[0:8])
    stream_b = Stream(out_b, 1, sems[8:16])
    stream_u = Stream(out_u, 1, sems[16:24])

    copies = tensor_scatter(plow_ref, inbox, s1, r1)
    scatter(up_part, in_u, 1, su, ru)
    wait_all(copies)
    tensor_reduce(inbox, full)
    copies = tensor_gather(full, s2, r2)

    @pl.when(core == 1)
    def _():
        arrived(in_u, ru)
        sum_adapters(ids, in_u, slice(0, RANK), out_u, chip)

        def one(m, total):
            return total + in_u[m, RANK:].astype(jnp.float32)

        total = lax.fori_loop(0, MEMBERS, one, jnp.zeros((RANK, HEAD), jnp.float32))
        out_u[chip, ADAPTERS] = total.astype(jnp.bfloat16)
        stream_u.start()

    wait_all(copies)
    low_grad = jnp.concatenate([full[b] for b in range(N_X)], axis=1)
    step = 4

    def columns(s, carry):
        cols = pl.ds(pl.multiple_of(s * (step * HEAD), step * HEAD), step * HEAD)
        product = matmul(low_grad, x_ref[:, cols]).astype(jnp.bfloat16)
        for j in range(step):
            tile = product[:, j * HEAD : (j + 1) * HEAD]
            down_a[s * step + j] = tile[: 2 * RANK]
            down_b[s * step + j] = tile[2 * RANK :]
        return carry

    lax.fori_loop(0, CHIPS // step, columns, 0)
    scatter(down_a, in_a, 0, sa, ra)
    scatter(down_b, in_b, 1, sb, rb)

    @pl.when(core == 0)
    def _():
        arrived(in_a, ra)
        sum_adapters(ids, in_a, slice(0, 2 * RANK), out_a, chip)
        stream_a.start()
        stream_a.spread()
        stream_a.pass_on()
        stream_a.finish()
        stream_b.receive()
        stream_u.receive()

    @pl.when(core == 1)
    def _():
        stream_u.spread()
        arrived(in_b, rb)
        sum_adapters(ids, in_b, slice(0, RANK), out_b, chip)
        stream_b.start()
        stream_u.pass_on()
        stream_b.spread()
        stream_b.pass_on()
        stream_u.finish()
        stream_b.finish()
        stream_a.receive()

    scatter_sent(up_part, in_u, 1, su, ru)
    scatter_sent(down_a, in_a, 0, sa, ra)
    scatter_sent(down_b, in_b, 1, sb, rb)


def widen_kernel(a_ref, b_ref, u_ref, kv_ref, down_ref, up_ref):
    for j in range(CHIPS):
        cols = slice(j * HEAD, (j + 1) * HEAD)
        down_ref[0, : 2 * RANK, cols] = a_ref[j, 0].astype(jnp.float32)
        down_ref[0, 2 * RANK :, cols] = b_ref[j, 0].astype(jnp.float32)
        up_ref[0, :, cols] = u_ref[j, 0].astype(jnp.float32)
    for kind in range(2):
        cols = slice((CHIPS + kind) * HEAD, (CHIPS + kind + 1) * HEAD)
        up_ref[0, :, cols] = kv_ref[kind, 0].astype(jnp.float32)


def per_device(x, base, grad, segments, ids, down, up):
    bf16, f32 = jnp.bfloat16, jnp.float32
    tokens, width = x.shape
    rows = KINDS * RANK
    blocks = tokens // BLOCK
    limit = 56 * 1024 * 1024

    low = pl.pallas_call(
        project_kernel,
        out_shape=jax.ShapeDtypeStruct((blocks, rows, BLOCK), bf16),
        in_specs=[smem(), vmem(), vmem()],
        out_specs=vmem(),
        scratch_shapes=[
            VMEM((blocks, rows, BLOCK), bf16),
            VMEM((N_TENSOR, rows, BLOCK), bf16),
            VMEM((blocks, rows, BLOCK), bf16),
            DMA((7,)), DMA((7,)), DMA((3,)), DMA((3,)),
        ],
        compiler_params=pltpu.CompilerParams(
            collective_id=0, has_side_effects=True, vmem_limit_bytes=limit
        ),
        name="project",
    )(ids, x, down)

    cols = base.shape[1]
    wide = STEP_HEADS * HEAD
    plow, up_part = pl.pallas_call(
        attention_kernel,
        grid=(blocks,),
        out_shape=(
            jax.ShapeDtypeStruct((blocks, rows, BLOCK), bf16),
            jax.ShapeDtypeStruct((CHIPS, 2 * RANK, HEAD), bf16),
        ),
        in_specs=[
            smem(),
            pl.BlockSpec((BLOCK, cols), lambda i: (i, 0)),
            pl.BlockSpec((BLOCK, HEADS * HEAD), lambda i: (i, 0)),
            vmem(), vmem(), vmem(),
        ],
        out_specs=(vmem(), vmem()),
        scratch_shapes=[
            VMEM((2 * BLOCK, HEAD), bf16),
            VMEM((2 * BLOCK, HEAD), bf16),
            VMEM((HEAD, 2 * BLOCK), bf16),
            VMEM((2 * BLOCK, BLOCK), f32),
            VMEM((wide, HEAD), bf16),
            VMEM((wide, HEAD), bf16),
            VMEM((tokens + BLOCK, HEAD), f32),
            VMEM((tokens + BLOCK, HEAD), f32),
            VMEM((RANK, HEADS * HEAD), f32),
            VMEM((RANK, BLOCK), f32),
            VMEM((RANK, cols), bf16),
        ],
        compiler_params=pltpu.CompilerParams(vmem_limit_bytes=limit),
        name="attention",
    )(ids, base, grad, segments, low, up)

    out_a, out_b, out_u = pl.pallas_call(
        adapters_kernel,
        out_shape=(
            jax.ShapeDtypeStruct((CHIPS, ADAPTERS, 2 * RANK, HEAD), bf16),
            jax.ShapeDtypeStruct((CHIPS, ADAPTERS, RANK, HEAD), bf16),
            jax.ShapeDtypeStruct((CHIPS, ADAPTERS + 1, RANK, HEAD), bf16),
        ),
        in_specs=[smem(), vmem(), vmem(), vmem()],
        out_specs=(vmem(), vmem(), vmem()),
        scratch_shapes=[
            VMEM((N_TENSOR, rows, BLOCK), bf16),
            VMEM((blocks, rows, BLOCK), bf16),
            DMA((7,)), DMA((7,)), DMA((3,)), DMA((3,)),
            VMEM((CHIPS, 2 * RANK, HEAD), bf16),
            VMEM((CHIPS, RANK, HEAD), bf16),
            VMEM((MEMBERS, 2 * RANK, HEAD), bf16),
            VMEM((MEMBERS, RANK, HEAD), bf16),
            VMEM((MEMBERS, 2 * RANK, HEAD), bf16),
            DMA((CHIPS,)), DMA((CHIPS,)), DMA((CHIPS,)),
            DMA, DMA, DMA,
        ] + STREAM_SEMS * 3,
        compiler_params=pltpu.CompilerParams(
            collective_id=1, has_side_effects=True, vmem_limit_bytes=limit
        ),
        name="adapters",
    )(ids, x, plow, up_part)

    return pl.pallas_call(
        widen_kernel,
        grid=(ADAPTERS,),
        out_shape=(
            jax.ShapeDtypeStruct((ADAPTERS, rows, width), f32),
            jax.ShapeDtypeStruct((ADAPTERS, RANK, cols), f32),
        ),
        in_specs=[
            pl.BlockSpec((CHIPS, 1, 2 * RANK, HEAD), lambda a: (0, a, 0, 0)),
            pl.BlockSpec((CHIPS, 1, RANK, HEAD), lambda a: (0, a, 0, 0)),
            pl.BlockSpec((CHIPS, 1, RANK, HEAD), lambda a: (0, a, 0, 0)),
            pl.BlockSpec((2, 1, RANK, HEAD), lambda a: (a, ADAPTERS, 0, 0)),
        ],
        out_specs=(
            pl.BlockSpec((1, rows, width), lambda a: (a, 0, 0)),
            pl.BlockSpec((1, RANK, cols), lambda a: (a, 0, 0)),
        ),
        compiler_params=pltpu.CompilerParams(vmem_limit_bytes=limit),
        name="widen",
    )(out_a, out_b, out_u, out_u)


def solution(mesh):
    placed = (
        P("dp", "tensor"),
        P("dp", "tensor"),
        P("dp", "tensor"),
        P("dp", None),
        P(),
        P(None, None, "tensor"),
        P(None, None, "tensor"),
    )
    return jax.shard_map(
        per_device,
        mesh=mesh,
        in_specs=placed,
        out_specs=(P(None, None, "tensor"), P(None, None, "tensor")),
        check_vma=False,
    )
```

```python
import functools
import math

import jax
import jax.numpy as jnp
from jax import lax
from jax.experimental import pallas as pl
from jax.experimental.pallas import tpu as pltpu
from jax.sharding import PartitionSpec as P

MESH = pl.DeviceIdType.MESH
VMEM = pltpu.VMEM
SMEM = pltpu.SMEM
DMA = pltpu.SemaphoreType.DMA

HEAD = 128
RANK = 16
HEADS = 16
KINDS = 3
BLOCK = 128
N_TENSOR = 8
N_X = 4
N_Y = 4
N_Z = 4
CHIPS = N_Y * N_Z
MEMBERS = 2 * CHIPS
ADAPTERS = 8
BLOCKS = 4
masked_score = -1e30

NT = (((1,), (1,)), ((), ()))
TN = (((0,), (0,)), ((), ()))
NN = (((1,), (0,)), ((), ()))


def matmul(a, b, dims=NN):
    return lax.dot_general(a, b, dims, preferred_element_type=jnp.float32)


def vmem():
    return pl.BlockSpec(memory_space=VMEM)


def smem():
    return pl.BlockSpec(memory_space=SMEM)


def greet_tensor(barrier):
    dp, me = lax.axis_index("dp"), lax.axis_index("tensor")
    for d in range(1, N_TENSOR):
        other = (me + d) % N_TENSOR
        pl.semaphore_signal(barrier, inc=1, device_id=(dp, other), device_id_type=MESH)


def tensor_scatter(part, inbox, send, recv):
    dp, me = lax.axis_index("dp"), lax.axis_index("tensor")
    copies = []
    for d in range(1, N_TENSOR):
        other = (me + d) % N_TENSOR
        copies.append(
            pltpu.make_async_remote_copy(
                src_ref=part.at[other % N_X],
                dst_ref=inbox.at[me],
                send_sem=send.at[d - 1],
                recv_sem=recv.at[d - 1],
                device_id=(dp, other),
                device_id_type=MESH,
            )
        )
        copies[-1].start()
    inbox[me] = part[me % N_X]
    return copies


def tensor_reduce(inbox, full):
    me = lax.axis_index("tensor")
    total = inbox[0].astype(jnp.float32)
    for i in range(1, N_TENSOR):
        total = total + inbox[i].astype(jnp.float32)
    full[me % N_X] = total.astype(jnp.bfloat16)


def tensor_gather(full, send, recv):
    dp, me = lax.axis_index("dp"), lax.axis_index("tensor")
    x, high = me % N_X, me // N_X
    copies = []
    for d in range(1, N_X):
        other = high * N_X + (x + d) % N_X
        copies.append(
            pltpu.make_async_remote_copy(
                src_ref=full.at[x],
                dst_ref=full.at[x],
                send_sem=send.at[d - 1],
                recv_sem=recv.at[d - 1],
                device_id=(dp, other),
                device_id_type=MESH,
            )
        )
        copies[-1].start()
    return copies


def received(copies):
    for copy in copies:
        copy.wait_recv()


def sent(copies):
    for copy in copies:
        copy.wait_send()


def split_dp():
    dp = lax.axis_index("dp")
    return dp // 2, dp % 2


def scatter(src, inbox, core_to, send, recv):
    dp, tensor = lax.axis_index("dp"), lax.axis_index("tensor")
    chip, core = split_dp()

    def one(k, carry):
        p = (chip + k) % CHIPS
        pltpu.make_async_remote_copy(
            src_ref=src.at[p],
            dst_ref=inbox.at[dp],
            send_sem=send.at[k],
            recv_sem=recv,
            device_id=(2 * p + core_to, tensor),
            device_id_type=MESH,
        ).start()
        return carry

    lax.fori_loop(1, CHIPS, one, 0)

    @pl.when(core == core_to)
    def _():
        pltpu.make_async_copy(src.at[chip], inbox.at[dp], recv).start()

    @pl.when(core != core_to)
    def _():
        one(0, 0)


def scatter_sent(src, inbox, core_to, send, recv):
    dp, tensor = lax.axis_index("dp"), lax.axis_index("tensor")
    chip, core = split_dp()

    def one(k, carry):
        pltpu.make_async_remote_copy(
            src_ref=src.at[chip],
            dst_ref=inbox.at[dp],
            send_sem=send.at[k],
            recv_sem=recv,
            device_id=(2 * chip + core_to, tensor),
            device_id_type=MESH,
        ).wait_send()
        return carry

    lax.fori_loop(1, CHIPS, one, 0)

    @pl.when(core != core_to)
    def _():
        one(0, 0)


def arrived(whole, sem):
    pltpu.make_async_copy(whole, whole, sem).wait()


def sum_adapters(ids, inbox, rows, out, slot):
    def one(m, sums):
        term = inbox[m, rows].astype(jnp.float32)
        adapter = ids[m]
        return tuple(
            sums[a] + term * (adapter == a).astype(jnp.float32) for a in range(ADAPTERS)
        )

    zero = jnp.zeros((rows.stop - rows.start, HEAD), jnp.float32)
    sums = lax.fori_loop(0, MEMBERS, one, (zero,) * ADAPTERS)
    for a in range(ADAPTERS):
        out[slot, a] = sums[a].astype(jnp.bfloat16)


class Stream:
    def __init__(self, out, owner, sems):
        self.out, self.owner = out, owner
        self.zs, self.zr, self.ys, self.yr, self.fs, self.fr, self.cs, self.cr = sems
        self.half = out.shape[1] // 2
        self.tensor = lax.axis_index("tensor")
        self.chip, self.core = split_dp()
        self.y, self.z = self.chip // N_Z, self.chip % N_Z

    def copy(self, slot, chip_to, core_to, send, recv, part=None):
        ref = self.out.at[slot] if part is None else self.out.at[slot, part]
        return pltpu.make_async_remote_copy(
            src_ref=ref,
            dst_ref=ref,
            send_sem=send,
            recv_sem=recv,
            device_id=(2 * chip_to + core_to, self.tensor),
            device_id_type=MESH,
        )

    def at(self, y, z):
        return (y % N_Y) * N_Z + z % N_Z

    def z_copy(self, d):
        return self.copy(
            self.chip, self.at(self.y, self.z + d), self.owner, self.zs.at[d - 1], self.zr.at[d - 1]
        )

    def y_copy(self, dz, side):
        to = self.at(self.y + (1 if side == 0 else 3), self.z)
        slot = self.at(self.y, self.z + N_Z - dz)
        n = 2 * dz + side
        return self.copy(slot, to, self.owner, self.ys.at[n], self.yr.at[n])

    def y_arrival(self, dz, side):
        n = 2 * dz + side
        return self.copy(
            self.y_slot(dz, side), self.chip, self.owner, self.ys.at[n], self.yr.at[n]
        )

    def y_slot(self, dz, side):
        return self.at(self.y + (3 if side == 0 else 1), self.z + N_Z - dz)

    def part(self, side):
        n = self.out.shape[1]
        return pl.ds(0, self.half) if side == 0 else pl.ds(self.half, n - self.half)

    def forward(self, dz, side):
        to = self.at(self.y + (1 if side == 0 else 3), self.z)
        slot = self.y_slot(dz, side)
        n = 2 * dz + side
        return self.copy(slot, to, self.owner, self.fs.at[n], self.fr.at[n], self.part(side))

    def forwarded(self, dz, side):
        slot = self.at(self.y + 2, self.z + N_Z - dz)
        n = 2 * dz + side
        return self.copy(slot, self.chip, self.owner, self.fs.at[n], self.fr.at[n], self.part(side))

    def twin(self, n, slot):
        return self.copy(slot, self.chip, 1 - self.owner, self.cs.at[n], self.cr)

    def start(self):
        for d in (1, 3, 2):
            self.z_copy(d).start()
        for side in range(2):
            self.y_copy(0, side).start()
        self.twin(0, self.chip).start()

    def spread(self):
        for dz in (1, 3, 2):
            self.z_copy(dz).wait_recv()
            for side in range(2):
                self.y_copy(dz, side).start()
            self.twin(dz, self.at(self.y, self.z + N_Z - dz)).start()

    def pass_on(self):
        for dz in (0, 1, 3, 2):
            for side in range(2):
                self.y_arrival(dz, side).wait_recv()
                self.forward(dz, side).start()
                self.twin(4 + 2 * dz + side, self.y_slot(dz, side)).start()

    def finish(self):
        for dz in (0, 1, 3, 2):
            for side in range(2):
                self.forwarded(dz, side).wait_recv()
            self.twin(12 + dz, self.at(self.y + 2, self.z + N_Z - dz)).start()
        for d in range(1, N_Z):
            self.z_copy(d).wait_send()
        for dz in range(N_Z):
            for side in range(2):
                self.y_copy(dz, side).wait_send()
                self.forward(dz, side).wait_send()
        for n in range(CHIPS):
            self.twin(n, self.chip).wait_send()

    def receive(self):
        arrived(self.out, self.cr)


STREAM_SEMS = [DMA((3,)), DMA((3,))] + [DMA((8,))] * 4 + [DMA((CHIPS,)), DMA]


def share(part, inbox, send, recv):
    dp, me = lax.axis_index("dp"), lax.axis_index("tensor")
    copies = []
    for d in range(1, N_TENSOR):
        copies.append(
            pltpu.make_async_remote_copy(
                src_ref=part,
                dst_ref=inbox.at[me],
                send_sem=send.at[d - 1],
                recv_sem=recv.at[d - 1],
                device_id=(dp, (me + d) % N_TENSOR),
                device_id_type=MESH,
            )
        )
        copies[-1].start()
    inbox[me] = part[...]
    return copies


def attend(base, grad, seg, low, up_half, keys, values, qs, gs, plow, gup, upout, mine, done):
    bf16, f32 = jnp.bfloat16, jnp.float32
    qcols = slice(0, HEADS * HEAD)
    kcols = slice(HEADS * HEAD, (HEADS + 1) * HEAD)
    vcols = slice((HEADS + 1) * HEAD, (HEADS + 2) * HEAD)
    scale = 1.0 / math.sqrt(HEAD)
    for b in range(BLOCKS):
        rows = slice(b * BLOCK, (b + 1) * BLOCK)
        low_k, low_v = low[b, RANK : 2 * RANK], low[b, 2 * RANK :]
        key = base[rows, kcols].astype(f32) + matmul(low_k, up_half[:, kcols], TN)
        value = base[rows, vcols].astype(f32) + matmul(low_v, up_half[:, vcols], TN)
        keys[rows] = key.astype(bf16)
        values[rows] = value.astype(bf16)
    u = lax.broadcasted_iota(jnp.int32, (BLOCK, BLOCK), 0)
    t = lax.broadcasted_iota(jnp.int32, (BLOCK, BLOCK), 1)
    docs = [
        jnp.broadcast_to(
            seg[:, b * BLOCK : (b + 1) * BLOCK].astype(f32), (BLOCK, BLOCK)
        )
        for b in range(BLOCKS)
    ]
    gup_k = jnp.zeros((RANK, HEAD), f32)
    gup_v = jnp.zeros((RANK, HEAD), f32)
    dk_next = dv_next = None
    for i in reversed(range(BLOCKS)):
        rows = slice(i * BLOCK, (i + 1) * BLOCK)
        first = max(i - 1, 0)
        window = slice(first * BLOCK, (i + 1) * BLOCK)
        mask = jnp.where((docs[i].T == docs[i]) & (u <= t), 0.0, masked_score)
        if first < i:
            before = jnp.where(docs[first].T == docs[i], 0.0, masked_score)
            mask = jnp.concatenate([before, mask], axis=0)
        mask = jnp.concatenate([mask] * HEADS, axis=1)
        key, value = keys[window], values[window]
        low_q = low[i, 0:RANK]
        up_q = up_half[:, qcols]
        q_wide = (base[rows, qcols].astype(f32) + matmul(low_q, up_q, TN)).astype(bf16)
        for h in range(HEADS):
            qs[i % 2, h * BLOCK : (h + 1) * BLOCK] = q_wide[:, h * HEAD : (h + 1) * HEAD]
        q, g = qs[i % 2], gs[i]
        scores = matmul(key, q, NT) * (scale * math.log2(math.e)) + mask
        top = jnp.max(scores, axis=0, keepdims=True)
        weights = jnp.exp2(scores - top)
        total = jnp.sum(weights, axis=0, keepdims=True)
        probs = weights * (1.0 / total)
        prob_grad = matmul(value, g, NT)
        row_dot = jnp.sum(probs * prob_grad, axis=0, keepdims=True)
        score_grad = (probs * (prob_grad - row_dot)).astype(bf16)
        dv = matmul(probs.astype(bf16), g)
        dk = matmul(score_grad, q)
        dq = (matmul(key.astype(f32).T.astype(bf16), score_grad) * scale).astype(bf16)
        dq = jnp.concatenate(
            [dq[:, h * BLOCK : (h + 1) * BLOCK] for h in range(HEADS)], axis=0
        )
        part_q = matmul(up_q, dq)
        if i == BLOCKS - 1:
            gup[...] = matmul(low_q, dq, NT)
            dk_own, dv_own = dk[BLOCK:], dv[BLOCK:]
        else:
            gup[...] += matmul(low_q, dq, NT)
            dk_own, dv_own = dk[-BLOCK:] + dk_next, dv[-BLOCK:] + dv_next
        dk_next, dv_next = dk[:BLOCK], dv[:BLOCK]
        dk_own, dv_own = (dk_own * scale).astype(bf16), dv_own.astype(bf16)
        plow[i, 0:RANK] = part_q.astype(bf16)
        plow[i, RANK : 2 * RANK] = matmul(up_half[:, kcols], dk_own, NT).astype(bf16)
        plow[i, 2 * RANK :] = matmul(up_half[:, vcols], dv_own, NT).astype(bf16)
        done(i)
        gup_k += matmul(low[i, RANK : 2 * RANK], dk_own)
        gup_v += matmul(low[i, 2 * RANK :], dv_own)
    gup_k, gup_v = gup_k * 0.5, gup_v * 0.5
    for j in range(CHIPS):
        upout[j, 0:RANK] = (gup[:, j * HEAD : (j + 1) * HEAD] * 0.5).astype(bf16)
        upout[j, RANK:] = ((gup_v if j % 2 else gup_k) * mine(j // 2)).astype(bf16)


def fused_kernel(
    ids, x_hbm, base_hbm, grad_hbm, seg, down_hbm, up_hbm, out_a, out_b, out_u,
    x_ref, base, grad, down_ref, up_ref, loads,
    part, inbox, low, s1, r1, s2, r2,
    up_half, keys, values, qs, gs, plow, gup, up_part, shared, s3, r3,
    down_a, down_b, in_a, in_b, in_u, sa, sb, su, ra, rb, ru, *sems,
):
    bf16, f32 = jnp.bfloat16, jnp.float32
    chip, core = split_dp()
    tensor, dp = lax.axis_index("tensor"), lax.axis_index("dp")
    fetch = [
        pltpu.make_async_copy(src, dst, loads.at[n])
        for n, (src, dst) in enumerate(
            [
                (down_hbm, down_ref), (x_hbm, x_ref), (up_hbm, up_ref),
                (grad_hbm, grad), (base_hbm, base),
            ]
        )
    ]
    for copy in fetch:
        copy.start()

    barrier = pltpu.get_barrier_semaphore()
    greet_tensor(barrier)

    def greet(k, carry):
        other = (dp + k) % MEMBERS
        pl.semaphore_signal(barrier, inc=1, device_id=(other, tensor), device_id_type=MESH)
        return carry

    lax.fori_loop(1, MEMBERS, greet, 0)

    adapter = ids[dp]
    fetch[0].wait()
    fetch[1].wait()
    partial_low = matmul(down_ref[adapter], x_ref[...], NT)
    for b in range(BLOCKS):
        part[b] = partial_low[:, b * BLOCK : (b + 1) * BLOCK].astype(bf16)
    pl.semaphore_wait(barrier, N_TENSOR - 1 + MEMBERS - 1)
    copies = tensor_scatter(part, inbox, s1, r1)
    fetch[2].wait()
    up_half[...] = (up_ref[adapter].astype(f32) * 0.5).astype(bf16)
    fetch[3].wait()
    for b in range(BLOCKS):
        for h in range(HEADS):
            tile = grad[b * BLOCK : (b + 1) * BLOCK, h * HEAD : (h + 1) * HEAD]
            gs[b, h * BLOCK : (h + 1) * BLOCK] = tile
    fetch[4].wait()
    received(copies)
    tensor_reduce(inbox, low)
    more = tensor_gather(low, s2, r2)
    received(more)
    copies = copies + more

    shares = []

    def done(i):
        shares.extend(share(plow.at[i], shared.at[i], s3.at[i], r3.at[i]))

    def mine(a):
        return (adapter == a).astype(f32)

    attend(base, grad, seg, low, up_half, keys, values, qs, gs, plow, gup, up_part, mine, done)
    scatter(up_part, in_u, 1, su, ru)

    received(shares)
    sums = []
    for b in range(BLOCKS):
        total = shared[b, 0].astype(f32)
        for n in range(1, N_TENSOR):
            total = total + shared[b, n].astype(f32)
        sums.append(total.astype(bf16))
    low_grad = jnp.concatenate(sums, axis=1)
    step = 4
    for s in range(CHIPS // step):
        product = matmul(low_grad, x_ref[:, s * step * HEAD : (s + 1) * step * HEAD]).astype(bf16)
        for j in range(step):
            tile = product[:, j * HEAD : (j + 1) * HEAD]
            down_a[s * step + j] = tile[: 2 * RANK]
            down_b[s * step + j] = tile[2 * RANK :]
    scatter(down_a, in_a, 0, sa, ra)
    scatter(down_b, in_b, 1, sb, rb)

    stream_a = Stream(out_a, 0, sems[0:8])
    stream_b = Stream(out_b, 1, sems[8:16])
    stream_u = Stream(out_u, 1, sems[16:24])

    @pl.when(core == 0)
    def _():
        arrived(in_a, ra)
        sum_adapters(ids, in_a, slice(0, 2 * RANK), out_a, chip)
        stream_a.start()
        stream_a.spread()
        stream_a.pass_on()
        stream_a.finish()
        stream_b.receive()
        stream_u.receive()

    @pl.when(core == 1)
    def _():
        arrived(in_u, ru)
        sum_adapters(ids, in_u, slice(0, RANK), out_u, chip)

        def one(m, total):
            return total + in_u[m, RANK:].astype(f32)

        total = lax.fori_loop(0, MEMBERS, one, jnp.zeros((RANK, HEAD), f32))
        out_u[chip, ADAPTERS] = total.astype(bf16)
        stream_u.start()
        arrived(in_b, rb)
        sum_adapters(ids, in_b, slice(0, RANK), out_b, chip)
        stream_b.start()
        stream_u.spread()
        stream_b.spread()
        stream_u.pass_on()
        stream_b.pass_on()
        stream_u.finish()
        stream_b.finish()
        stream_a.receive()

    sent(copies + shares)
    scatter_sent(up_part, in_u, 1, su, ru)
    scatter_sent(down_a, in_a, 0, sa, ra)
    scatter_sent(down_b, in_b, 1, sb, rb)


def widen_kernel(a_ref, b_ref, u_ref, kv_ref, down_ref, up_ref):
    for j in range(CHIPS):
        cols = slice(j * HEAD, (j + 1) * HEAD)
        down_ref[0, : 2 * RANK, cols] = a_ref[j, 0].astype(jnp.float32)
        down_ref[0, 2 * RANK :, cols] = b_ref[j, 0].astype(jnp.float32)
        up_ref[0, :, cols] = u_ref[j, 0].astype(jnp.float32)
    for kind in range(2):
        cols = slice((CHIPS + kind) * HEAD, (CHIPS + kind + 1) * HEAD)
        up_ref[0, :, cols] = kv_ref[kind, 0].astype(jnp.float32)


def hbm():
    return pl.BlockSpec(memory_space=pl.ANY)


def per_device(x, base, grad, segments, ids, down, up):
    bf16, f32 = jnp.bfloat16, jnp.float32
    tokens, width = x.shape
    cols = base.shape[1]
    rows = KINDS * RANK
    limit = 58 * 1024 * 1024
    out_a, out_b, out_u = pl.pallas_call(
        fused_kernel,
        out_shape=(
            jax.ShapeDtypeStruct((CHIPS, ADAPTERS, 2 * RANK, HEAD), bf16),
            jax.ShapeDtypeStruct((CHIPS, ADAPTERS, RANK, HEAD), bf16),
            jax.ShapeDtypeStruct((CHIPS, ADAPTERS + 1, RANK, HEAD), bf16),
        ),
        in_specs=[smem(), hbm(), hbm(), hbm(), vmem(), hbm(), hbm()],
        out_specs=(vmem(), vmem(), vmem()),
        scratch_shapes=[
            VMEM(x.shape, bf16), VMEM(base.shape, bf16), VMEM(grad.shape, bf16),
            VMEM(down.shape, bf16), VMEM(up.shape, bf16), DMA((5,)),
            VMEM((BLOCKS, rows, BLOCK), bf16),
            VMEM((N_TENSOR, rows, BLOCK), bf16),
            VMEM((BLOCKS, rows, BLOCK), bf16),
            DMA((7,)), DMA((7,)), DMA((3,)), DMA((3,)),
            VMEM((RANK, cols), bf16),
            VMEM((tokens, HEAD), bf16),
            VMEM((tokens, HEAD), bf16),
            VMEM((2, HEADS * BLOCK, HEAD), bf16),
            VMEM((BLOCKS, HEADS * BLOCK, HEAD), bf16),
            VMEM((BLOCKS, rows, BLOCK), bf16),
            VMEM((RANK, HEADS * HEAD), f32),
            VMEM((CHIPS, 2 * RANK, HEAD), bf16),
            VMEM((BLOCKS, N_TENSOR, rows, BLOCK), bf16),
            DMA((BLOCKS, 7)), DMA((BLOCKS, 7)),
            VMEM((CHIPS, 2 * RANK, HEAD), bf16),
            VMEM((CHIPS, RANK, HEAD), bf16),
            VMEM((MEMBERS, 2 * RANK, HEAD), bf16),
            VMEM((MEMBERS, RANK, HEAD), bf16),
            VMEM((MEMBERS, 2 * RANK, HEAD), bf16),
            DMA((CHIPS,)), DMA((CHIPS,)), DMA((CHIPS,)),
            DMA, DMA, DMA,
        ] + STREAM_SEMS * 3,
        compiler_params=pltpu.CompilerParams(
            collective_id=0, has_side_effects=True, vmem_limit_bytes=limit
        ),
        name="fused",
    )(ids.reshape(-1), x, base, grad, segments, down, up)

    return pl.pallas_call(
        widen_kernel,
        grid=(ADAPTERS,),
        out_shape=(
            jax.ShapeDtypeStruct((ADAPTERS, rows, width), f32),
            jax.ShapeDtypeStruct((ADAPTERS, RANK, cols), f32),
        ),
        in_specs=[
            pl.BlockSpec((CHIPS, 1, 2 * RANK, HEAD), lambda a: (0, a, 0, 0)),
            pl.BlockSpec((CHIPS, 1, RANK, HEAD), lambda a: (0, a, 0, 0)),
            pl.BlockSpec((CHIPS, 1, RANK, HEAD), lambda a: (0, a, 0, 0)),
            pl.BlockSpec((2, 1, RANK, HEAD), lambda a: (a, ADAPTERS, 0, 0)),
        ],
        out_specs=(
            pl.BlockSpec((1, rows, width), lambda a: (a, 0, 0)),
            pl.BlockSpec((1, RANK, cols), lambda a: (a, 0, 0)),
        ),
        compiler_params=pltpu.CompilerParams(vmem_limit_bytes=limit),
        name="widen",
    )(out_a, out_b, out_u, out_u)


def solution(mesh):
    placed = (
        P("dp", "tensor"),
        P("dp", "tensor"),
        P("dp", "tensor"),
        P("dp", None),
        P(),
        P(None, None, "tensor"),
        P(None, None, "tensor"),
    )
    return jax.shard_map(
        per_device,
        mesh=mesh,
        in_specs=placed,
        out_specs=(P(None, None, "tensor"), P(None, None, "tensor")),
        check_vma=False,
    )
```

```python
import functools
import math

import jax
import jax.numpy as jnp
from jax import lax
from jax.experimental import pallas as pl
from jax.experimental.pallas import tpu as pltpu
from jax.sharding import PartitionSpec as P

MESH = pl.DeviceIdType.MESH
VMEM = pltpu.VMEM
SMEM = pltpu.SMEM
DMA = pltpu.SemaphoreType.DMA

HEAD = 128
RANK = 16
HEADS = 16
KINDS = 3
BLOCK = 128
N_TENSOR = 8
N_X = 4
N_Y = 4
N_Z = 4
CHIPS = N_Y * N_Z
MEMBERS = 2 * CHIPS
ADAPTERS = 8
BLOCKS = 4
STEP_ADAPTERS = 4
masked_score = -1e30

NT = (((1,), (1,)), ((), ()))
TN = (((0,), (0,)), ((), ()))
NN = (((1,), (0,)), ((), ()))


def matmul(a, b, dims=NN):
    return lax.dot_general(a, b, dims, preferred_element_type=jnp.float32)


def vmem():
    return pl.BlockSpec(memory_space=VMEM)


def smem():
    return pl.BlockSpec(memory_space=SMEM)


def greet_tensor(barrier):
    dp, me = lax.axis_index("dp"), lax.axis_index("tensor")
    for d in range(1, N_TENSOR):
        other = (me + d) % N_TENSOR
        pl.semaphore_signal(barrier, inc=1, device_id=(dp, other), device_id_type=MESH)


def tensor_scatter(part, inbox, send, recv):
    dp, me = lax.axis_index("dp"), lax.axis_index("tensor")
    copies = []
    for d in range(1, N_TENSOR):
        other = (me + d) % N_TENSOR
        copies.append(
            pltpu.make_async_remote_copy(
                src_ref=part.at[other % N_X],
                dst_ref=inbox.at[me],
                send_sem=send.at[d - 1],
                recv_sem=recv.at[d - 1],
                device_id=(dp, other),
                device_id_type=MESH,
            )
        )
        copies[-1].start()
    inbox[me] = part[me % N_X]
    return copies


def tensor_reduce(inbox, full):
    me = lax.axis_index("tensor")
    total = inbox[0].astype(jnp.float32)
    for i in range(1, N_TENSOR):
        total = total + inbox[i].astype(jnp.float32)
    full[me % N_X] = total.astype(jnp.bfloat16)


def tensor_gather(full, send, recv):
    dp, me = lax.axis_index("dp"), lax.axis_index("tensor")
    x, high = me % N_X, me // N_X
    copies = []
    for d in range(1, N_X):
        other = high * N_X + (x + d) % N_X
        copies.append(
            pltpu.make_async_remote_copy(
                src_ref=full.at[x],
                dst_ref=full.at[x],
                send_sem=send.at[d - 1],
                recv_sem=recv.at[d - 1],
                device_id=(dp, other),
                device_id_type=MESH,
            )
        )
        copies[-1].start()
    return copies


def received(copies):
    for copy in copies:
        copy.wait_recv()


def sent(copies):
    for copy in copies:
        copy.wait_send()


def split_dp():
    dp = lax.axis_index("dp")
    return dp // 2, dp % 2


def piece(src, inbox, p, core_to, send, recv):
    dp, tensor = lax.axis_index("dp"), lax.axis_index("tensor")
    return pltpu.make_async_remote_copy(
        src_ref=src.at[p],
        dst_ref=inbox.at[dp],
        send_sem=send,
        recv_sem=recv,
        device_id=(2 * p + core_to, tensor),
        device_id_type=MESH,
    )


def own_piece(src, inbox, core_to, send, recv):
    chip, core = split_dp()

    @pl.when(core == core_to)
    def _():
        pltpu.make_async_copy(src.at[chip], inbox.at[lax.axis_index("dp")], recv).start()

    @pl.when(core != core_to)
    def _():
        piece(src, inbox, chip, core_to, send.at[0], recv).start()


def scatter(src, inbox, core_to, send, recv):
    chip, _ = split_dp()

    def one(k, carry):
        piece(src, inbox, (chip + k) % CHIPS, core_to, send.at[k], recv).start()
        return carry

    lax.fori_loop(1, CHIPS, one, 0)
    own_piece(src, inbox, core_to, send, recv)


def scatter_sent(src, inbox, core_to, send, recv):
    chip, core = split_dp()

    def one(k, carry):
        piece(src, inbox, chip, core_to, send.at[k], recv).wait_send()
        return carry

    lax.fori_loop(1, CHIPS, one, 0)

    @pl.when(core != core_to)
    def _():
        one(0, 0)


def arrived(whole, sem):
    pltpu.make_async_copy(whole, whole, sem).wait()


def sum_adapters(ids, inbox, rows, out, slot):
    def one(m, sums):
        term = inbox[m, rows].astype(jnp.float32)
        adapter = ids[m]
        return tuple(
            sums[a] + term * (adapter == a).astype(jnp.float32) for a in range(ADAPTERS)
        )

    zero = jnp.zeros((rows.stop - rows.start, HEAD), jnp.float32)
    sums = lax.fori_loop(0, MEMBERS, one, (zero,) * ADAPTERS)
    for a in range(ADAPTERS):
        out[slot, a] = sums[a].astype(jnp.bfloat16)


class Stream:
    def __init__(self, buf, out, owner, sems):
        self.buf, self.out, self.owner = buf, out, owner
        self.zs, self.zr, self.ys, self.yr, self.cs, self.cr, self.ks = sems
        self.tensor = lax.axis_index("tensor")
        self.chip, self.core = split_dp()
        self.y, self.z = self.chip // N_Z, self.chip % N_Z

    def copy(self, slot, chip_to, core_to, send, recv, dst=None):
        return pltpu.make_async_remote_copy(
            src_ref=self.buf.at[slot],
            dst_ref=(self.buf if dst is None else dst).at[slot],
            send_sem=send,
            recv_sem=recv,
            device_id=(2 * chip_to + core_to, self.tensor),
            device_id_type=MESH,
        )

    def at(self, dy, dz):
        return ((self.y + dy + N_Y) % N_Y) * N_Z + (self.z + dz + N_Z) % N_Z

    def nearest_first(self):
        z, high = self.z, self.z // 2
        sources = (z + 1 - 2 * (z % 2), 2 - high, 3 * (1 - high))
        return [(z - source + N_Z) % N_Z for source in sources]

    def z_copy(self, d):
        return self.copy(
            self.chip, self.at(0, d), self.owner, self.zs.at[d - 1], self.zr.at[d - 1]
        )

    def y_copy(self, dz, dy):
        n = 3 * dz + dy - 1
        return self.copy(self.at(0, -dz), self.at(dy, 0), self.owner, self.ys.at[n], self.yr.at[n])

    def twin(self, n, slot):
        return self.copy(
            slot, self.chip, 1 - self.owner, self.cs.at[n], self.cr, self.out
        )

    def deliver(self, n, slot):
        self.twin(n, slot).start()
        pltpu.make_async_copy(self.buf.at[slot], self.out.at[slot], self.ks).start()

    def y_sends(self, dz):
        for dy in (2, 1, 3):
            self.y_copy(dz, dy).start()
        self.deliver(dz, self.at(0, -dz))

    def start(self):
        for d in (2, 1, 3):
            self.z_copy(d).start()
        self.y_sends(0)

    def spread(self):
        for dz in self.nearest_first():
            self.z_copy(dz).wait_recv()
            self.y_sends(dz)

    def finish(self):
        for dz in [0] + self.nearest_first():
            for dy in (1, 3, 2):
                self.y_copy(dz, dy).wait_recv()
                self.deliver(4 + 3 * dz + dy - 1, self.at(-dy, -dz))

    def sent(self):
        for d in range(1, N_Z):
            self.z_copy(d).wait_send()
        for dz in range(N_Z):
            for dy in range(1, N_Y):
                self.y_copy(dz, dy).wait_send()
        for n in range(CHIPS):
            self.twin(n, self.chip).wait_send()
        pltpu.make_async_copy(self.buf, self.out, self.ks).wait()

    def receive(self):
        arrived(self.out, self.cr)


STREAM_SEMS = [DMA((3,)), DMA((3,)), DMA((12,)), DMA((12,)), DMA((CHIPS,)), DMA, DMA]


def share(part, inbox, send, recv):
    dp, me = lax.axis_index("dp"), lax.axis_index("tensor")
    copies = []
    for d in range(1, N_TENSOR):
        copies.append(
            pltpu.make_async_remote_copy(
                src_ref=part,
                dst_ref=inbox.at[me],
                send_sem=send.at[d - 1],
                recv_sem=recv.at[d - 1],
                device_id=(dp, (me + d) % N_TENSOR),
                device_id_type=MESH,
            )
        )
        copies[-1].start()
    inbox[me] = part[...]
    return copies


def attend(base, grad, seg, low, up_half, keys, values, qs, gs, plow, gup, upout, mine, done):
    bf16, f32 = jnp.bfloat16, jnp.float32
    qcols = slice(0, HEADS * HEAD)
    kcols = slice(HEADS * HEAD, (HEADS + 1) * HEAD)
    vcols = slice((HEADS + 1) * HEAD, (HEADS + 2) * HEAD)
    scale = 1.0 / math.sqrt(HEAD)
    for b in range(BLOCKS):
        rows = slice(b * BLOCK, (b + 1) * BLOCK)
        low_k, low_v = low[b, RANK : 2 * RANK], low[b, 2 * RANK :]
        key = base[rows, kcols].astype(f32) + matmul(low_k, up_half[:, kcols], TN)
        value = base[rows, vcols].astype(f32) + matmul(low_v, up_half[:, vcols], TN)
        keys[rows] = key.astype(bf16)
        values[rows] = value.astype(bf16)
    u = lax.broadcasted_iota(jnp.int32, (BLOCK, BLOCK), 0)
    t = lax.broadcasted_iota(jnp.int32, (BLOCK, BLOCK), 1)
    docs = [
        jnp.broadcast_to(
            seg[:, b * BLOCK : (b + 1) * BLOCK].astype(f32), (BLOCK, BLOCK)
        )
        for b in range(BLOCKS)
    ]
    gup_k = jnp.zeros((RANK, HEAD), f32)
    gup_v = jnp.zeros((RANK, HEAD), f32)
    dk_next = dv_next = None
    for i in reversed(range(BLOCKS)):
        rows = slice(i * BLOCK, (i + 1) * BLOCK)
        first = max(i - 1, 0)
        window = slice(first * BLOCK, (i + 1) * BLOCK)
        mask = jnp.where((docs[i].T == docs[i]) & (u <= t), 0.0, masked_score)
        if first < i:
            before = jnp.where(docs[first].T == docs[i], 0.0, masked_score)
            mask = jnp.concatenate([before, mask], axis=0)
        mask = jnp.concatenate([mask] * HEADS, axis=1)
        key, value = keys[window], values[window]
        low_q = low[i, 0:RANK]
        up_q = up_half[:, qcols]
        q_wide = (base[rows, qcols].astype(f32) + matmul(low_q, up_q, TN)).astype(bf16)
        for h in range(HEADS):
            qs[i % 2, h * BLOCK : (h + 1) * BLOCK] = q_wide[:, h * HEAD : (h + 1) * HEAD]
        q, g = qs[i % 2], gs[i]
        scores = matmul(key, q, NT) * (scale * math.log2(math.e)) + mask
        top = jnp.max(scores, axis=0, keepdims=True)
        weights = jnp.exp2(scores - top)
        total = jnp.sum(weights, axis=0, keepdims=True)
        probs = weights * (1.0 / total)
        prob_grad = matmul(value, g, NT)
        row_dot = jnp.sum(probs * prob_grad, axis=0, keepdims=True)
        score_grad = (probs * (prob_grad - row_dot)).astype(bf16)
        dv = matmul(probs.astype(bf16), g)
        dk = matmul(score_grad, q)
        dq = (matmul(key.astype(f32).T.astype(bf16), score_grad) * scale).astype(bf16)
        dq = jnp.concatenate(
            [dq[:, h * BLOCK : (h + 1) * BLOCK] for h in range(HEADS)], axis=0
        )
        part_q = matmul(up_q, dq)
        if i == BLOCKS - 1:
            gup[...] = matmul(low_q, dq, NT)
            dk_own, dv_own = dk[BLOCK:], dv[BLOCK:]
        else:
            gup[...] += matmul(low_q, dq, NT)
            dk_own, dv_own = dk[-BLOCK:] + dk_next, dv[-BLOCK:] + dv_next
        dk_next, dv_next = dk[:BLOCK], dv[:BLOCK]
        dk_own, dv_own = (dk_own * scale).astype(bf16), dv_own.astype(bf16)
        plow[i, 0:RANK] = part_q.astype(bf16)
        plow[i, RANK : 2 * RANK] = matmul(up_half[:, kcols], dk_own, NT).astype(bf16)
        plow[i, 2 * RANK :] = matmul(up_half[:, vcols], dv_own, NT).astype(bf16)
        done(i)
        gup_k += matmul(low[i, RANK : 2 * RANK], dk_own)
        gup_v += matmul(low[i, 2 * RANK :], dv_own)
    gup_k, gup_v = gup_k * 0.5, gup_v * 0.5
    for j in range(CHIPS):
        upout[j, 0:RANK] = (gup[:, j * HEAD : (j + 1) * HEAD] * 0.5).astype(bf16)
        upout[j, RANK:] = ((gup_v if j % 2 else gup_k) * mine(j // 2)).astype(bf16)


def fused_kernel(
    ids, x_hbm, base_hbm, grad_hbm, seg, down_hbm, up_hbm, out_a, out_b, out_u,
    x_ref, base, grad, down_ref, up_ref, loads,
    part, inbox, low, s1, r1, s2, r2,
    up_half, keys, values, qs, gs, plow, gup, up_part, shared, s3, r3,
    down_early, down_a, down_b, in_a, in_b, in_u, sa, sb, su, ra, rb, ru,
    buf_a, buf_b, buf_u, *sems,
):
    bf16, f32 = jnp.bfloat16, jnp.float32
    chip, core = split_dp()
    tensor, dp = lax.axis_index("tensor"), lax.axis_index("dp")
    fetch = [
        pltpu.make_async_copy(src, dst, loads.at[n])
        for n, (src, dst) in enumerate(
            [
                (down_hbm, down_ref), (x_hbm, x_ref), (up_hbm, up_ref),
                (grad_hbm, grad), (base_hbm, base),
            ]
        )
    ]
    for copy in fetch:
        copy.start()

    barrier = pltpu.get_barrier_semaphore()
    greet_tensor(barrier)

    def greet(k, carry):
        other = (dp + k) % MEMBERS
        pl.semaphore_signal(barrier, inc=1, device_id=(other, tensor), device_id_type=MESH)
        return carry

    lax.fori_loop(1, MEMBERS, greet, 0)

    adapter = ids[dp]
    fetch[0].wait()
    fetch[1].wait()
    partial_low = matmul(down_ref[adapter], x_ref[...], NT)
    for b in range(BLOCKS):
        part[b] = partial_low[:, b * BLOCK : (b + 1) * BLOCK].astype(bf16)
    pl.semaphore_wait(barrier, N_TENSOR - 1 + MEMBERS - 1)
    copies = tensor_scatter(part, inbox, s1, r1)
    fetch[2].wait()
    up_half[...] = (up_ref[adapter].astype(f32) * 0.5).astype(bf16)
    fetch[3].wait()
    for b in range(BLOCKS):
        for h in range(HEADS):
            tile = grad[b * BLOCK : (b + 1) * BLOCK, h * HEAD : (h + 1) * HEAD]
            gs[b, h * BLOCK : (h + 1) * BLOCK] = tile
    fetch[4].wait()
    received(copies)
    tensor_reduce(inbox, low)
    more = tensor_gather(low, s2, r2)
    received(more)
    copies = copies + more

    shares = {}

    def done(i):
        shares[i] = share(plow.at[i], shared.at[i], s3.at[i], r3.at[i])

    def mine(a):
        return (adapter == a).astype(f32)

    attend(base, grad, seg, low, up_half, keys, values, qs, gs, plow, gup, up_part, mine, done)
    scatter(up_part, in_u, 1, su, ru)

    def low_grad(b):
        received(shares[b])
        total = shared[b, 0].astype(f32)
        for n in range(1, N_TENSOR):
            total = total + shared[b, n].astype(f32)
        return total.astype(bf16)

    early = jnp.concatenate([low_grad(b) for b in range(1, BLOCKS)], axis=1)
    wide = N_Z * HEAD
    for s in range(N_Y):
        cols = slice(s * wide, (s + 1) * wide)
        down_early[:, cols] = matmul(early, x_ref[BLOCK:, cols])
    late = low_grad(0)
    y, z = chip // N_Z, chip % N_Z
    for s, dy in enumerate((2, 1, 3, 0)):
        there = (y + dy) % N_Y
        cols = pl.ds(pl.multiple_of(there * wide, wide), wide)
        product = (matmul(late, x_ref[:BLOCK, cols]) + down_early[:, cols]).astype(bf16)
        for j in range(N_Z):
            tile = product[:, j * HEAD : (j + 1) * HEAD]
            down_a[there * N_Z + j] = tile[: 2 * RANK]
            down_b[there * N_Z + j] = tile[2 * RANK :]
        for j in range(N_Z):
            if dy:
                p = there * N_Z + (1 - z // 2) * (3 - j) + (z // 2) * j
            else:
                p = there * N_Z + (z + j) % N_Z
            n = (4 + 4 * s + j) if dy else j
            if dy or j:
                piece(down_a, in_a, p, 0, sa.at[n], ra).start()
                piece(down_b, in_b, p, 1, sb.at[n], rb).start()
    own_piece(down_a, in_a, 0, sa, ra)
    own_piece(down_b, in_b, 1, sb, rb)

    stream_a = Stream(buf_a, out_a, 0, sems[0:7])
    stream_b = Stream(buf_b, out_b, 1, sems[7:14])
    stream_u = Stream(buf_u, out_u, 1, sems[14:21])

    @pl.when(core == 0)
    def _():
        arrived(in_a, ra)
        sum_adapters(ids, in_a, slice(0, 2 * RANK), buf_a, chip)
        stream_a.start()
        stream_a.spread()
        stream_a.finish()
        stream_a.sent()
        stream_b.receive()
        stream_u.receive()

    @pl.when(core == 1)
    def _():
        arrived(in_u, ru)
        sum_adapters(ids, in_u, slice(0, RANK), buf_u, chip)

        def one(m, total):
            return total + in_u[m, RANK:].astype(f32)

        total = lax.fori_loop(0, MEMBERS, one, jnp.zeros((RANK, HEAD), f32))
        buf_u[chip, ADAPTERS] = total.astype(bf16)
        stream_u.start()
        arrived(in_b, rb)
        sum_adapters(ids, in_b, slice(0, RANK), buf_b, chip)
        stream_b.start()
        stream_u.spread()
        stream_b.spread()
        stream_u.finish()
        stream_b.finish()
        stream_u.sent()
        stream_b.sent()
        stream_a.receive()

    sent(copies + sum(shares.values(), []))
    scatter_sent(up_part, in_u, 1, su, ru)
    scatter_sent(down_a, in_a, 0, sa, ra)
    scatter_sent(down_b, in_b, 1, sb, rb)


def widen_kernel(a_ref, b_ref, u_ref, kv_ref, down_ref, up_ref):
    for j in range(CHIPS):
        cols = slice(j * HEAD, (j + 1) * HEAD)
        down_ref[:, : 2 * RANK, cols] = a_ref[j].astype(jnp.float32)
        down_ref[:, 2 * RANK :, cols] = b_ref[j].astype(jnp.float32)
        up_ref[:, :, cols] = u_ref[j].astype(jnp.float32)
    for kind in range(2):
        cols = slice((CHIPS + kind) * HEAD, (CHIPS + kind + 1) * HEAD)
        for a in range(STEP_ADAPTERS):
            up_ref[a, :, cols] = kv_ref[2 * a + kind, 0].astype(jnp.float32)


def hbm():
    return pl.BlockSpec(memory_space=pl.ANY)


def per_device(x, base, grad, segments, ids, down, up):
    bf16, f32 = jnp.bfloat16, jnp.float32
    tokens, width = x.shape
    cols = base.shape[1]
    rows = KINDS * RANK
    limit = 58 * 1024 * 1024
    out_a, out_b, out_u = pl.pallas_call(
        fused_kernel,
        out_shape=(
            jax.ShapeDtypeStruct((CHIPS, ADAPTERS, 2 * RANK, HEAD), bf16),
            jax.ShapeDtypeStruct((CHIPS, ADAPTERS, RANK, HEAD), bf16),
            jax.ShapeDtypeStruct((CHIPS, ADAPTERS + 1, RANK, HEAD), bf16),
        ),
        in_specs=[smem(), hbm(), hbm(), hbm(), vmem(), hbm(), hbm()],
        out_specs=(hbm(), hbm(), hbm()),
        scratch_shapes=[
            VMEM(x.shape, bf16), VMEM(base.shape, bf16), VMEM(grad.shape, bf16),
            VMEM(down.shape, bf16), VMEM(up.shape, bf16), DMA((5,)),
            VMEM((BLOCKS, rows, BLOCK), bf16),
            VMEM((N_TENSOR, rows, BLOCK), bf16),
            VMEM((BLOCKS, rows, BLOCK), bf16),
            DMA((7,)), DMA((7,)), DMA((3,)), DMA((3,)),
            VMEM((RANK, cols), bf16),
            VMEM((tokens, HEAD), bf16),
            VMEM((tokens, HEAD), bf16),
            VMEM((2, HEADS * BLOCK, HEAD), bf16),
            VMEM((BLOCKS, HEADS * BLOCK, HEAD), bf16),
            VMEM((BLOCKS, rows, BLOCK), bf16),
            VMEM((RANK, HEADS * HEAD), f32),
            VMEM((CHIPS, 2 * RANK, HEAD), bf16),
            VMEM((BLOCKS, N_TENSOR, rows, BLOCK), bf16),
            DMA((BLOCKS, 7)), DMA((BLOCKS, 7)),
            VMEM((rows, width), f32),
            VMEM((CHIPS, 2 * RANK, HEAD), bf16),
            VMEM((CHIPS, RANK, HEAD), bf16),
            VMEM((MEMBERS, 2 * RANK, HEAD), bf16),
            VMEM((MEMBERS, RANK, HEAD), bf16),
            VMEM((MEMBERS, 2 * RANK, HEAD), bf16),
            DMA((CHIPS,)), DMA((CHIPS,)), DMA((CHIPS,)),
            DMA, DMA, DMA,
            VMEM((CHIPS, ADAPTERS, 2 * RANK, HEAD), bf16),
            VMEM((CHIPS, ADAPTERS, RANK, HEAD), bf16),
            VMEM((CHIPS, ADAPTERS + 1, RANK, HEAD), bf16),
        ] + STREAM_SEMS * 3,
        compiler_params=pltpu.CompilerParams(
            collective_id=0, has_side_effects=True, vmem_limit_bytes=limit
        ),
        name="fused",
    )(ids.reshape(-1), x, base, grad, segments, down, up)

    return pl.pallas_call(
        widen_kernel,
        grid=(ADAPTERS // STEP_ADAPTERS,),
        out_shape=(
            jax.ShapeDtypeStruct((ADAPTERS, rows, width), f32),
            jax.ShapeDtypeStruct((ADAPTERS, RANK, cols), f32),
        ),
        in_specs=[
            pl.BlockSpec((CHIPS, STEP_ADAPTERS, 2 * RANK, HEAD), lambda a: (0, a, 0, 0)),
            pl.BlockSpec((CHIPS, STEP_ADAPTERS, RANK, HEAD), lambda a: (0, a, 0, 0)),
            pl.BlockSpec((CHIPS, STEP_ADAPTERS, RANK, HEAD), lambda a: (0, a, 0, 0)),
            pl.BlockSpec((2 * STEP_ADAPTERS, 1, RANK, HEAD), lambda a: (a, ADAPTERS, 0, 0)),
        ],
        out_specs=(
            pl.BlockSpec((STEP_ADAPTERS, rows, width), lambda a: (a, 0, 0)),
            pl.BlockSpec((STEP_ADAPTERS, RANK, cols), lambda a: (a, 0, 0)),
        ),
        compiler_params=pltpu.CompilerParams(vmem_limit_bytes=limit),
        name="widen",
    )(out_a, out_b, out_u, out_u)


def solution(mesh):
    placed = (
        P("dp", "tensor"),
        P("dp", "tensor"),
        P("dp", "tensor"),
        P("dp", None),
        P(),
        P(None, None, "tensor"),
        P(None, None, "tensor"),
    )
    return jax.shard_map(
        per_device,
        mesh=mesh,
        in_specs=placed,
        out_specs=(P(None, None, "tensor"), P(None, None, "tensor")),
        check_vma=False,
    )
```

```python
import functools
import math

import jax
import jax.numpy as jnp
from jax import lax
from jax.experimental import pallas as pl
from jax.experimental.pallas import tpu as pltpu
from jax.sharding import PartitionSpec as P

MESH = pl.DeviceIdType.MESH
VMEM = pltpu.VMEM
SMEM = pltpu.SMEM
DMA = pltpu.SemaphoreType.DMA

HEAD = 128
RANK = 16
HEADS = 16
KINDS = 3
BLOCK = 128
N_TENSOR = 8
N_X = 4
N_Y = 4
N_Z = 4
CHIPS = N_Y * N_Z
MEMBERS = 2 * CHIPS
ADAPTERS = 8
BLOCKS = 4
masked_score = -1e30

NT = (((1,), (1,)), ((), ()))
TN = (((0,), (0,)), ((), ()))
NN = (((1,), (0,)), ((), ()))


def matmul(a, b, dims=NN):
    return lax.dot_general(a, b, dims, preferred_element_type=jnp.float32)


def vmem():
    return pl.BlockSpec(memory_space=VMEM)


def smem():
    return pl.BlockSpec(memory_space=SMEM)


def greet_tensor(barrier):
    dp, me = lax.axis_index("dp"), lax.axis_index("tensor")
    for d in range(1, N_TENSOR):
        other = (me + d) % N_TENSOR
        pl.semaphore_signal(barrier, inc=1, device_id=(dp, other), device_id_type=MESH)


def tensor_scatter(part, inbox, send, recv):
    dp, me = lax.axis_index("dp"), lax.axis_index("tensor")
    copies = []
    for d in range(1, N_TENSOR):
        other = (me + d) % N_TENSOR
        copies.append(
            pltpu.make_async_remote_copy(
                src_ref=part.at[other % N_X],
                dst_ref=inbox.at[me],
                send_sem=send.at[d - 1],
                recv_sem=recv.at[d - 1],
                device_id=(dp, other),
                device_id_type=MESH,
            )
        )
        copies[-1].start()
    inbox[me] = part[me % N_X]
    return copies


def tensor_reduce(inbox, full):
    me = lax.axis_index("tensor")
    total = inbox[0].astype(jnp.float32)
    for i in range(1, N_TENSOR):
        total = total + inbox[i].astype(jnp.float32)
    full[me % N_X] = total.astype(jnp.bfloat16)


def tensor_gather(full, send, recv):
    dp, me = lax.axis_index("dp"), lax.axis_index("tensor")
    x, high = me % N_X, me // N_X
    copies = []
    for d in range(1, N_X):
        other = high * N_X + (x + d) % N_X
        copies.append(
            pltpu.make_async_remote_copy(
                src_ref=full.at[x],
                dst_ref=full.at[x],
                send_sem=send.at[d - 1],
                recv_sem=recv.at[d - 1],
                device_id=(dp, other),
                device_id_type=MESH,
            )
        )
        copies[-1].start()
    return copies


def received(copies):
    for copy in copies:
        copy.wait_recv()


def sent(copies):
    for copy in copies:
        copy.wait_send()


def split_dp():
    dp = lax.axis_index("dp")
    return dp // 2, dp % 2


def piece(src, inbox, p, core_to, send, recv):
    dp, tensor = lax.axis_index("dp"), lax.axis_index("tensor")
    return pltpu.make_async_remote_copy(
        src_ref=src.at[p],
        dst_ref=inbox.at[dp],
        send_sem=send,
        recv_sem=recv,
        device_id=(2 * p + core_to, tensor),
        device_id_type=MESH,
    )


def own_piece(src, inbox, core_to, send, recv):
    chip, core = split_dp()

    @pl.when(core == core_to)
    def _():
        pltpu.make_async_copy(src.at[chip], inbox.at[lax.axis_index("dp")], recv).start()

    @pl.when(core != core_to)
    def _():
        piece(src, inbox, chip, core_to, send.at[0], recv).start()


def scatter(src, inbox, core_to, send, recv):
    chip, _ = split_dp()

    def one(k, carry):
        piece(src, inbox, (chip + k) % CHIPS, core_to, send.at[k], recv).start()
        return carry

    lax.fori_loop(1, CHIPS, one, 0)
    own_piece(src, inbox, core_to, send, recv)


def scatter_sent(src, inbox, core_to, send, recv):
    chip, core = split_dp()

    def one(k, carry):
        piece(src, inbox, chip, core_to, send.at[k], recv).wait_send()
        return carry

    lax.fori_loop(1, CHIPS, one, 0)

    @pl.when(core != core_to)
    def _():
        one(0, 0)


def arrived(whole, sem):
    pltpu.make_async_copy(whole, whole, sem).wait()


def sum_adapters(ids, inbox, rows, out, slot):
    def one(m, sums):
        term = inbox[m, rows].astype(jnp.float32)
        adapter = ids[m]
        return tuple(
            sums[a] + term * (adapter == a).astype(jnp.float32) for a in range(ADAPTERS)
        )

    zero = jnp.zeros((rows.stop - rows.start, HEAD), jnp.float32)
    sums = lax.fori_loop(0, MEMBERS, one, (zero,) * ADAPTERS)
    for a in range(ADAPTERS):
        out[slot, a] = sums[a].astype(jnp.bfloat16)


class Stream:
    def __init__(self, buf, out, owner, sems):
        self.buf, self.out, self.owner = buf, out, owner
        self.zs, self.zr, self.ys, self.yr, self.cs, self.cr, self.ks = sems
        self.tensor = lax.axis_index("tensor")
        self.chip, self.core = split_dp()
        self.y, self.z = self.chip // N_Z, self.chip % N_Z

    def copy(self, slot, chip_to, core_to, send, recv, dst=None):
        return pltpu.make_async_remote_copy(
            src_ref=self.buf.at[slot],
            dst_ref=(self.buf if dst is None else dst).at[slot],
            send_sem=send,
            recv_sem=recv,
            device_id=(2 * chip_to + core_to, self.tensor),
            device_id_type=MESH,
        )

    def at(self, dy, dz):
        return ((self.y + dy + N_Y) % N_Y) * N_Z + (self.z + dz + N_Z) % N_Z

    def nearest_first(self):
        z, high = self.z, self.z // 2
        sources = (z + 1 - 2 * (z % 2), 2 - high, 3 * (1 - high))
        return [(z - source + N_Z) % N_Z for source in sources]

    def z_copy(self, d):
        return self.copy(
            self.chip, self.at(0, d), self.owner, self.zs.at[d - 1], self.zr.at[d - 1]
        )

    def y_copy(self, dz, dy):
        n = 3 * dz + dy - 1
        return self.copy(self.at(0, -dz), self.at(dy, 0), self.owner, self.ys.at[n], self.yr.at[n])

    def twin(self, n, slot):
        return self.copy(
            slot, self.chip, 1 - self.owner, self.cs.at[n], self.cr, self.out
        )

    def deliver(self, n, slot):
        self.twin(n, slot).start()
        pltpu.make_async_copy(self.buf.at[slot], self.out.at[slot], self.ks).start()

    def y_sends(self, dz):
        for dy in (2, 1, 3):
            self.y_copy(dz, dy).start()
        self.deliver(dz, self.at(0, -dz))

    def start(self):
        for d in (2, 1, 3):
            self.z_copy(d).start()
        self.y_sends(0)

    def spread(self):
        for dz in self.nearest_first():
            self.z_copy(dz).wait_recv()
            self.y_sends(dz)

    def finish(self):
        for dz in [0] + self.nearest_first():
            for dy in (1, 3, 2):
                self.y_copy(dz, dy).wait_recv()
                self.deliver(4 + 3 * dz + dy - 1, self.at(-dy, -dz))

    def sent(self):
        for d in range(1, N_Z):
            self.z_copy(d).wait_send()
        for dz in range(N_Z):
            for dy in range(1, N_Y):
                self.y_copy(dz, dy).wait_send()
        for n in range(CHIPS):
            self.twin(n, self.chip).wait_send()
        pltpu.make_async_copy(self.buf, self.out, self.ks).wait()

    def receive(self):
        arrived(self.out, self.cr)


STREAM_SEMS = [DMA((3,)), DMA((3,)), DMA((12,)), DMA((12,)), DMA((CHIPS,)), DMA, DMA]


def share(part, inbox, send, recv):
    dp, me = lax.axis_index("dp"), lax.axis_index("tensor")
    copies = []
    for d in range(1, N_TENSOR):
        copies.append(
            pltpu.make_async_remote_copy(
                src_ref=part,
                dst_ref=inbox.at[me],
                send_sem=send.at[d - 1],
                recv_sem=recv.at[d - 1],
                device_id=(dp, (me + d) % N_TENSOR),
                device_id_type=MESH,
            )
        )
        copies[-1].start()
    inbox[me] = part[...]
    return copies


def fill_masks(seg, masks):
    u = lax.broadcasted_iota(jnp.int32, (BLOCK, BLOCK), 0)
    t = lax.broadcasted_iota(jnp.int32, (BLOCK, BLOCK), 1)
    docs = [
        jnp.broadcast_to(
            seg[:, b * BLOCK : (b + 1) * BLOCK].astype(jnp.float32), (BLOCK, BLOCK)
        )
        for b in range(BLOCKS)
    ]
    for i in range(BLOCKS):
        masks[i, BLOCK:] = jnp.where((docs[i].T == docs[i]) & (u <= t), 0.0, masked_score)
        if i:
            masks[i, :BLOCK] = jnp.where(docs[i - 1].T == docs[i], 0.0, masked_score)


ORDER = "A3 B3 A2 C3 B2 A1 C2 B1 A0 C1 B0 C0".split()


def attend(base, masks, low, up_half, keys, values, gs, dqs, plow, upout, mine, done):
    bf16, f32 = jnp.bfloat16, jnp.float32
    qcols = slice(0, HEADS * HEAD)
    kcols = slice(HEADS * HEAD, (HEADS + 1) * HEAD)
    vcols = slice((HEADS + 1) * HEAD, (HEADS + 2) * HEAD)
    scale = 1.0 / math.sqrt(HEAD)
    low_q, low_k, low_v = (
        jnp.concatenate([low[b, n * RANK : (n + 1) * RANK] for b in range(BLOCKS)], axis=1)
        for n in range(KINDS)
    )
    keys[...] = (base[:, kcols].astype(f32) + matmul(low_k, up_half[:, kcols], TN)).astype(bf16)
    values[...] = (base[:, vcols].astype(f32) + matmul(low_v, up_half[:, vcols], TN)).astype(bf16)
    up_q = up_half[:, qcols]
    held, grads, next_dk, next_dv = {}, {}, {}, {}
    own_k, own_v = {}, {}

    def window(i):
        return slice(max(i - 1, 0) * BLOCK, (i + 1) * BLOCK)

    def stage_a(i):
        rows = slice(i * BLOCK, (i + 1) * BLOCK)
        q_wide = base[rows, qcols].astype(f32) + matmul(low[i, 0:RANK], up_q, TN)
        q_wide = q_wide.astype(bf16)
        q = jnp.concatenate([q_wide[:, h * HEAD : (h + 1) * HEAD] for h in range(HEADS)], axis=0)
        held[i] = q, matmul(keys[window(i)], q, NT)

    def stage_b(i):
        q, scores = held.pop(i)
        mask = masks[i] if i else masks[0, BLOCK:]
        mask = jnp.concatenate([mask] * HEADS, axis=1)
        scores = scores * (scale * math.log2(math.e)) + mask
        top = jnp.max(scores, axis=0, keepdims=True)
        weights = jnp.exp2(scores - top)
        total = jnp.sum(weights, axis=0, keepdims=True)
        probs = weights * (1.0 / total)
        prob_grad = matmul(values[window(i)], gs[i], NT)
        row_dot = jnp.sum(probs * prob_grad, axis=0, keepdims=True)
        score_grad = (probs * (prob_grad - row_dot)).astype(bf16)
        grads[i] = q, probs.astype(bf16), score_grad

    def stage_c(i):
        q, probs, score_grad = grads.pop(i)
        dk = matmul(score_grad, q)
        dv = matmul(probs, gs[i])
        key = keys[window(i)]
        dq = (matmul(key.astype(f32).T.astype(bf16), score_grad) * scale).astype(bf16)
        dq = jnp.concatenate(
            [dq[:, h * BLOCK : (h + 1) * BLOCK] for h in range(HEADS)], axis=0
        )
        dqs[:, i * BLOCK : (i + 1) * BLOCK] = dq
        dk_own, dv_own = dk[-BLOCK:], dv[-BLOCK:]
        if i < BLOCKS - 1:
            dk_own, dv_own = dk_own + next_dk.pop(i), dv_own + next_dv.pop(i)
        if i:
            next_dk[i - 1], next_dv[i - 1] = dk[:BLOCK], dv[:BLOCK]
        own_k[i], own_v[i] = (dk_own * scale).astype(bf16), dv_own.astype(bf16)
        plow[i, 0:RANK] = matmul(up_q, dq).astype(bf16)
        plow[i, RANK : 2 * RANK] = matmul(up_half[:, kcols], own_k[i], NT).astype(bf16)
        plow[i, 2 * RANK :] = matmul(up_half[:, vcols], own_v[i], NT).astype(bf16)
        done(i)

    stages = {"A": stage_a, "B": stage_b, "C": stage_c}
    for item in ORDER:
        stages[item[0]](int(item[1]))

    gup = matmul(low_q, dqs[...], NT) * 0.5
    gup_k = sum(matmul(low[b, RANK : 2 * RANK], own_k[b]) for b in range(BLOCKS)) * 0.5
    gup_v = sum(matmul(low[b, 2 * RANK :], own_v[b]) for b in range(BLOCKS)) * 0.5
    for j in range(CHIPS):
        upout[j, 0:RANK] = gup[:, j * HEAD : (j + 1) * HEAD].astype(bf16)
        upout[j, RANK:] = ((gup_v if j % 2 else gup_k) * mine(j // 2)).astype(bf16)


def fused_kernel(
    ids_hbm, x_hbm, base_hbm, grad_hbm, seg_hbm, down_hbm, up_hbm, out_a, out_b, out_u,
    ids, x_ref, base, grad, seg, down_ref, up_ref, masks, loads,
    part, inbox, low, s1, r1, s2, r2,
    up_half, keys, values, gs, dqs, plow, up_part, shared, s3, r3,
    down_early, down_a, down_b, in_a, in_b, in_u, sa, sb, su, ra, rb, ru,
    buf_a, buf_b, buf_u, *sems,
):
    bf16, f32 = jnp.bfloat16, jnp.float32
    chip, core = split_dp()
    tensor, dp = lax.axis_index("tensor"), lax.axis_index("dp")
    fetch = [
        pltpu.make_async_copy(src, dst, loads.at[n])
        for n, (src, dst) in enumerate(
            [
                (ids_hbm, ids), (down_hbm, down_ref), (x_hbm, x_ref), (up_hbm, up_ref),
                (grad_hbm, grad), (base_hbm, base), (seg_hbm, seg),
            ]
        )
    ]
    for copy in fetch:
        copy.start()

    barrier = pltpu.get_barrier_semaphore()
    greet_tensor(barrier)

    def greet(k, carry):
        other = (dp + k) % MEMBERS
        pl.semaphore_signal(barrier, inc=1, device_id=(other, tensor), device_id_type=MESH)
        return carry

    lax.fori_loop(1, MEMBERS, greet, 0)

    fetch[0].wait()
    adapter = ids[dp]
    fetch[1].wait()
    fetch[2].wait()
    partial_low = matmul(down_ref[adapter], x_ref[...], NT)
    for b in range(BLOCKS):
        part[b] = partial_low[:, b * BLOCK : (b + 1) * BLOCK].astype(bf16)
    pl.semaphore_wait(barrier, N_TENSOR - 1 + MEMBERS - 1)
    copies = tensor_scatter(part, inbox, s1, r1)
    fetch[3].wait()
    up_half[...] = (up_ref[adapter].astype(f32) * 0.5).astype(bf16)
    fetch[6].wait()
    fill_masks(seg, masks)
    fetch[4].wait()
    for b in range(BLOCKS):
        for h in range(HEADS):
            tile = grad[b * BLOCK : (b + 1) * BLOCK, h * HEAD : (h + 1) * HEAD]
            gs[b, h * BLOCK : (h + 1) * BLOCK] = tile
    fetch[5].wait()
    received(copies)
    tensor_reduce(inbox, low)
    more = tensor_gather(low, s2, r2)
    received(more)
    copies = copies + more

    shares = {}

    def done(i):
        shares[i] = share(plow.at[i], shared.at[i], s3.at[i], r3.at[i])

    def mine(a):
        return (adapter == a).astype(f32)

    attend(base, masks, low, up_half, keys, values, gs, dqs, plow, up_part, mine, done)
    scatter(up_part, in_u, 1, su, ru)

    def low_grad(b):
        received(shares[b])
        total = shared[b, 0].astype(f32)
        for n in range(1, N_TENSOR):
            total = total + shared[b, n].astype(f32)
        return total.astype(bf16)

    early = jnp.concatenate([low_grad(b) for b in range(1, BLOCKS)], axis=1)
    wide = N_Z * HEAD
    for s in range(N_Y):
        cols = slice(s * wide, (s + 1) * wide)
        down_early[:, cols] = matmul(early, x_ref[BLOCK:, cols])
    late = low_grad(0)
    y, z = chip // N_Z, chip % N_Z
    for s, dy in enumerate((2, 1, 3, 0)):
        there = (y + dy) % N_Y
        cols = pl.ds(pl.multiple_of(there * wide, wide), wide)
        product = (matmul(late, x_ref[:BLOCK, cols]) + down_early[:, cols]).astype(bf16)
        for j in range(N_Z):
            tile = product[:, j * HEAD : (j + 1) * HEAD]
            down_a[there * N_Z + j] = tile[: 2 * RANK]
            down_b[there * N_Z + j] = tile[2 * RANK :]
        for j in range(N_Z):
            if dy:
                p = there * N_Z + (1 - z // 2) * (3 - j) + (z // 2) * j
            else:
                p = there * N_Z + (z + j) % N_Z
            n = (4 + 4 * s + j) if dy else j
            if dy or j:
                piece(down_a, in_a, p, 0, sa.at[n], ra).start()
                piece(down_b, in_b, p, 1, sb.at[n], rb).start()
    own_piece(down_a, in_a, 0, sa, ra)
    own_piece(down_b, in_b, 1, sb, rb)

    stream_a = Stream(buf_a, out_a, 0, sems[0:7])
    stream_b = Stream(buf_b, out_b, 1, sems[7:14])
    stream_u = Stream(buf_u, out_u, 1, sems[14:21])

    @pl.when(core == 0)
    def _():
        arrived(in_a, ra)
        sum_adapters(ids, in_a, slice(0, 2 * RANK), buf_a, chip)
        stream_a.start()
        stream_a.spread()
        stream_a.finish()
        stream_a.sent()
        stream_b.receive()
        stream_u.receive()

    @pl.when(core == 1)
    def _():
        arrived(in_u, ru)
        sum_adapters(ids, in_u, slice(0, RANK), buf_u, chip)

        def one(m, total):
            return total + in_u[m, RANK:].astype(f32)

        total = lax.fori_loop(0, MEMBERS, one, jnp.zeros((RANK, HEAD), f32))
        buf_u[chip, ADAPTERS] = total.astype(bf16)
        stream_u.start()
        arrived(in_b, rb)
        sum_adapters(ids, in_b, slice(0, RANK), buf_b, chip)
        stream_b.start()
        stream_u.spread()
        stream_b.spread()
        stream_u.finish()
        stream_b.finish()
        stream_u.sent()
        stream_b.sent()
        stream_a.receive()

    sent(copies + sum(shares.values(), []))
    scatter_sent(up_part, in_u, 1, su, ru)
    scatter_sent(down_a, in_a, 0, sa, ra)
    scatter_sent(down_b, in_b, 1, sb, rb)


def widen_kernel(a_hbm, b_hbm, u_hbm, down_hbm, up_hbm, a_ref, b_ref, u_ref, down, up, sems):
    def fetches(a):
        return [
            pltpu.make_async_copy(src.at[:, a], dst.at[:, a], sems.at[n, a])
            for n, (src, dst) in enumerate([(a_hbm, a_ref), (b_hbm, b_ref), (u_hbm, u_ref)])
        ]

    pairs = pltpu.make_async_copy(
        u_hbm.at[:, ADAPTERS], u_ref.at[:, ADAPTERS], sems.at[2, ADAPTERS]
    )
    pairs.start()
    for a in range(ADAPTERS):
        for copy in fetches(a):
            copy.start()
    pairs.wait()
    stores = []
    for a in range(ADAPTERS):
        for copy in fetches(a):
            copy.wait()
        for j in range(CHIPS):
            cols = slice(j * HEAD, (j + 1) * HEAD)
            down[a, : 2 * RANK, cols] = a_ref[j, a].astype(jnp.float32)
            down[a, 2 * RANK :, cols] = b_ref[j, a].astype(jnp.float32)
            up[a, :, cols] = u_ref[j, a].astype(jnp.float32)
        for kind in range(2):
            cols = slice((CHIPS + kind) * HEAD, (CHIPS + kind + 1) * HEAD)
            up[a, :, cols] = u_ref[2 * a + kind, ADAPTERS].astype(jnp.float32)
        for n, (src, dst) in enumerate([(down, down_hbm), (up, up_hbm)]):
            stores.append(pltpu.make_async_copy(src.at[a], dst.at[a], sems.at[3 + n, a]))
            stores[-1].start()
    for copy in stores:
        copy.wait()


def hbm():
    return pl.BlockSpec(memory_space=pl.ANY)


def per_device(x, base, grad, segments, ids, down, up):
    bf16, f32 = jnp.bfloat16, jnp.float32
    tokens, width = x.shape
    cols = base.shape[1]
    rows = KINDS * RANK
    limit = 58 * 1024 * 1024
    out_a, out_b, out_u = pl.pallas_call(
        fused_kernel,
        out_shape=(
            jax.ShapeDtypeStruct((CHIPS, ADAPTERS, 2 * RANK, HEAD), bf16),
            jax.ShapeDtypeStruct((CHIPS, ADAPTERS, RANK, HEAD), bf16),
            jax.ShapeDtypeStruct((CHIPS, ADAPTERS + 1, RANK, HEAD), bf16),
        ),
        in_specs=[hbm()] * 7,
        out_specs=(hbm(), hbm(), hbm()),
        scratch_shapes=[
            SMEM((MEMBERS,), jnp.int32),
            VMEM(x.shape, bf16), VMEM(base.shape, bf16), VMEM(grad.shape, bf16),
            VMEM(segments.shape, jnp.int32),
            VMEM(down.shape, bf16), VMEM(up.shape, bf16),
            VMEM((BLOCKS, 2 * BLOCK, BLOCK), f32), DMA((7,)),
            VMEM((BLOCKS, rows, BLOCK), bf16),
            VMEM((N_TENSOR, rows, BLOCK), bf16),
            VMEM((BLOCKS, rows, BLOCK), bf16),
            DMA((7,)), DMA((7,)), DMA((3,)), DMA((3,)),
            VMEM((RANK, cols), bf16),
            VMEM((tokens, HEAD), bf16),
            VMEM((tokens, HEAD), bf16),
            VMEM((BLOCKS, HEADS * BLOCK, HEAD), bf16),
            VMEM((HEADS * HEAD, tokens), bf16),
            VMEM((BLOCKS, rows, BLOCK), bf16),
            VMEM((CHIPS, 2 * RANK, HEAD), bf16),
            VMEM((BLOCKS, N_TENSOR, rows, BLOCK), bf16),
            DMA((BLOCKS, 7)), DMA((BLOCKS, 7)),
            VMEM((rows, width), f32),
            VMEM((CHIPS, 2 * RANK, HEAD), bf16),
            VMEM((CHIPS, RANK, HEAD), bf16),
            VMEM((MEMBERS, 2 * RANK, HEAD), bf16),
            VMEM((MEMBERS, RANK, HEAD), bf16),
            VMEM((MEMBERS, 2 * RANK, HEAD), bf16),
            DMA((CHIPS,)), DMA((CHIPS,)), DMA((CHIPS,)),
            DMA, DMA, DMA,
            VMEM((CHIPS, ADAPTERS, 2 * RANK, HEAD), bf16),
            VMEM((CHIPS, ADAPTERS, RANK, HEAD), bf16),
            VMEM((CHIPS, ADAPTERS + 1, RANK, HEAD), bf16),
        ] + STREAM_SEMS * 3,
        compiler_params=pltpu.CompilerParams(
            collective_id=0, has_side_effects=True, vmem_limit_bytes=limit
        ),
        name="fused",
    )(ids.reshape(-1), x, base, grad, segments, down, up)

    return pl.pallas_call(
        widen_kernel,
        out_shape=(
            jax.ShapeDtypeStruct((ADAPTERS, rows, width), f32),
            jax.ShapeDtypeStruct((ADAPTERS, RANK, cols), f32),
        ),
        in_specs=[hbm()] * 3,
        out_specs=(hbm(), hbm()),
        scratch_shapes=[
            VMEM(out_a.shape, bf16), VMEM(out_b.shape, bf16), VMEM(out_u.shape, bf16),
            VMEM((ADAPTERS, rows, width), f32),
            VMEM((ADAPTERS, RANK, cols), f32),
            DMA((5, ADAPTERS + 1)),
        ],
        compiler_params=pltpu.CompilerParams(vmem_limit_bytes=limit),
        name="widen",
    )(out_a, out_b, out_u)


def solution(mesh):
    placed = (
        P("dp", "tensor"),
        P("dp", "tensor"),
        P("dp", "tensor"),
        P("dp", None),
        P(),
        P(None, None, "tensor"),
        P(None, None, "tensor"),
    )
    return jax.shard_map(
        per_device,
        mesh=mesh,
        in_specs=placed,
        out_specs=(P(None, None, "tensor"), P(None, None, "tensor")),
        check_vma=False,
    )
```

```python
import functools
import math

import jax
import jax.numpy as jnp
from jax import lax
from jax.experimental import pallas as pl
from jax.experimental.pallas import tpu as pltpu
from jax.sharding import PartitionSpec as P

MESH = pl.DeviceIdType.MESH
VMEM = pltpu.VMEM
SMEM = pltpu.SMEM
DMA = pltpu.SemaphoreType.DMA

HEAD = 128
RANK = 16
HEADS = 16
KINDS = 3
BLOCK = 128
N_TENSOR = 8
N_X = 4
N_Y = 4
N_Z = 4
CHIPS = N_Y * N_Z
MEMBERS = 2 * CHIPS
ADAPTERS = 8
BLOCKS = 4
masked_score = -1e30

NT = (((1,), (1,)), ((), ()))
TN = (((0,), (0,)), ((), ()))
NN = (((1,), (0,)), ((), ()))


def matmul(a, b, dims=NN):
    return lax.dot_general(a, b, dims, preferred_element_type=jnp.float32)


def vmem():
    return pl.BlockSpec(memory_space=VMEM)


def smem():
    return pl.BlockSpec(memory_space=SMEM)


FAR_FIRST = ((1, 2), (1, 1), (1, 3), (1, 0), (0, 2), (0, 1), (0, 3))


def tensor_peers():
    me = lax.axis_index("tensor")
    x, high = me % N_X, me // N_X
    return [((high + dh) % 2) * N_X + (x + dx) % N_X for dh, dx in FAR_FIRST]


def greet_tensor(barrier):
    dp = lax.axis_index("dp")
    for other in tensor_peers():
        pl.semaphore_signal(barrier, inc=1, device_id=(dp, other), device_id_type=MESH)


def tensor_scatter(part, inbox, send, recv):
    dp, me = lax.axis_index("dp"), lax.axis_index("tensor")
    copies = []
    for n, other in enumerate(tensor_peers()):
        copies.append(
            pltpu.make_async_remote_copy(
                src_ref=part.at[other % N_X],
                dst_ref=inbox.at[me],
                send_sem=send.at[n],
                recv_sem=recv.at[n],
                device_id=(dp, other),
                device_id_type=MESH,
            )
        )
        copies[-1].start()
    inbox[me] = part[me % N_X]
    return copies


def tensor_reduce(inbox, full):
    me = lax.axis_index("tensor")
    total = inbox[0].astype(jnp.float32)
    for i in range(1, N_TENSOR):
        total = total + inbox[i].astype(jnp.float32)
    full[me % N_X] = total.astype(jnp.bfloat16)


def tensor_gather(full, send, recv):
    dp, me = lax.axis_index("dp"), lax.axis_index("tensor")
    x, high = me % N_X, me // N_X
    copies = []
    for d in range(1, N_X):
        other = high * N_X + (x + d) % N_X
        copies.append(
            pltpu.make_async_remote_copy(
                src_ref=full.at[x],
                dst_ref=full.at[x],
                send_sem=send.at[d - 1],
                recv_sem=recv.at[d - 1],
                device_id=(dp, other),
                device_id_type=MESH,
            )
        )
        copies[-1].start()
    return copies


def received(copies):
    for copy in copies:
        copy.wait_recv()


def sent(copies):
    for copy in copies:
        copy.wait_send()


def split_dp():
    dp = lax.axis_index("dp")
    return dp // 2, dp % 2


def piece(src, inbox, p, core_to, send, recv):
    dp, tensor = lax.axis_index("dp"), lax.axis_index("tensor")
    return pltpu.make_async_remote_copy(
        src_ref=src.at[p],
        dst_ref=inbox.at[dp],
        send_sem=send,
        recv_sem=recv,
        device_id=(2 * p + core_to, tensor),
        device_id_type=MESH,
    )


def own_piece(src, inbox, core_to, send, recv):
    chip, core = split_dp()

    @pl.when(core == core_to)
    def _():
        pltpu.make_async_copy(src.at[chip], inbox.at[lax.axis_index("dp")], recv).start()

    @pl.when(core != core_to)
    def _():
        piece(src, inbox, chip, core_to, send.at[0], recv).start()


def scatter(src, inbox, core_to, send, recv):
    chip, _ = split_dp()

    def one(k, carry):
        piece(src, inbox, (chip + k) % CHIPS, core_to, send.at[k], recv).start()
        return carry

    lax.fori_loop(1, CHIPS, one, 0)
    own_piece(src, inbox, core_to, send, recv)


def scatter_sent(src, inbox, core_to, send, recv):
    chip, core = split_dp()

    def one(k, carry):
        piece(src, inbox, chip, core_to, send.at[k], recv).wait_send()
        return carry

    lax.fori_loop(1, CHIPS, one, 0)

    @pl.when(core != core_to)
    def _():
        one(0, 0)


def arrived(whole, sem):
    pltpu.make_async_copy(whole, whole, sem).wait()


def sum_adapters(ids, inbox, rows, out, slot):
    def one(m, sums):
        term = inbox[m, rows].astype(jnp.float32)
        adapter = ids[m]
        return tuple(
            sums[a] + term * (adapter == a).astype(jnp.float32) for a in range(ADAPTERS)
        )

    zero = jnp.zeros((rows.stop - rows.start, HEAD), jnp.float32)
    sums = lax.fori_loop(0, MEMBERS, one, (zero,) * ADAPTERS)
    for a in range(ADAPTERS):
        out[slot, a] = sums[a].astype(jnp.bfloat16)


class Stream:
    def __init__(self, buf, out, owner, sems):
        self.buf, self.out, self.owner = buf, out, owner
        self.zs, self.zr, self.ys, self.yr, self.cs, self.cr, self.ks = sems
        self.tensor = lax.axis_index("tensor")
        self.chip, self.core = split_dp()
        self.y, self.z = self.chip // N_Z, self.chip % N_Z

    def copy(self, slot, chip_to, core_to, send, recv, dst=None):
        return pltpu.make_async_remote_copy(
            src_ref=self.buf.at[slot],
            dst_ref=(self.buf if dst is None else dst).at[slot],
            send_sem=send,
            recv_sem=recv,
            device_id=(2 * chip_to + core_to, self.tensor),
            device_id_type=MESH,
        )

    def at(self, dy, dz):
        return ((self.y + dy + N_Y) % N_Y) * N_Z + (self.z + dz + N_Z) % N_Z

    def nearest_first(self):
        z, high = self.z, self.z // 2
        sources = (z + 1 - 2 * (z % 2), 2 - high, 3 * (1 - high))
        return [(z - source + N_Z) % N_Z for source in sources]

    def z_copy(self, d):
        return self.copy(
            self.chip, self.at(0, d), self.owner, self.zs.at[d - 1], self.zr.at[d - 1]
        )

    def y_copy(self, dz, dy):
        n = 3 * dz + dy - 1
        return self.copy(self.at(0, -dz), self.at(dy, 0), self.owner, self.ys.at[n], self.yr.at[n])

    def twin(self, n, slot):
        return self.copy(
            slot, self.chip, 1 - self.owner, self.cs.at[n], self.cr, self.out
        )

    def deliver(self, n, slot):
        self.twin(n, slot).start()
        pltpu.make_async_copy(self.buf.at[slot], self.out.at[slot], self.ks).start()

    def y_sends(self, dz):
        for dy in (2, 1, 3):
            self.y_copy(dz, dy).start()
        self.deliver(dz, self.at(0, -dz))

    def start(self):
        for d in (2, 1, 3):
            self.z_copy(d).start()
        self.y_sends(0)

    def spread(self):
        for dz in self.nearest_first():
            self.z_copy(dz).wait_recv()
            self.y_sends(dz)

    def finish(self):
        for dz in [0] + self.nearest_first():
            for dy in (1, 3, 2):
                self.y_copy(dz, dy).wait_recv()
                self.deliver(4 + 3 * dz + dy - 1, self.at(-dy, -dz))

    def sent(self):
        for d in range(1, N_Z):
            self.z_copy(d).wait_send()
        for dz in range(N_Z):
            for dy in range(1, N_Y):
                self.y_copy(dz, dy).wait_send()
        for n in range(CHIPS):
            self.twin(n, self.chip).wait_send()
        pltpu.make_async_copy(self.buf, self.out, self.ks).wait()

    def receive(self):
        arrived(self.out, self.cr)


STREAM_SEMS = [DMA((3,)), DMA((3,)), DMA((12,)), DMA((12,)), DMA((CHIPS,)), DMA, DMA]


def share(part, inbox, send, recv):
    dp, me = lax.axis_index("dp"), lax.axis_index("tensor")
    copies = []
    for n, other in enumerate(tensor_peers()):
        copies.append(
            pltpu.make_async_remote_copy(
                src_ref=part,
                dst_ref=inbox.at[me],
                send_sem=send.at[n],
                recv_sem=recv.at[n],
                device_id=(dp, other),
                device_id_type=MESH,
            )
        )
        copies[-1].start()
    inbox[me] = part[...]
    return copies


def fill_masks(seg, masks):
    u = lax.broadcasted_iota(jnp.int32, (BLOCK, BLOCK), 0)
    t = lax.broadcasted_iota(jnp.int32, (BLOCK, BLOCK), 1)
    docs = [
        jnp.broadcast_to(
            seg[:, b * BLOCK : (b + 1) * BLOCK].astype(jnp.float32), (BLOCK, BLOCK)
        )
        for b in range(BLOCKS)
    ]
    for i in range(BLOCKS):
        masks[i, BLOCK:] = jnp.where((docs[i].T == docs[i]) & (u <= t), 0.0, masked_score)
        if i:
            masks[i, :BLOCK] = jnp.where(docs[i - 1].T == docs[i], 0.0, masked_score)


ORDER = "A3 B3 A2 C3 B2 A1 C2 B1 A0 C1 B0 C0".split()


def attend(base, masks, low, up_half, keys, values, gs, dqs, plow, upout, mine, done):
    bf16, f32 = jnp.bfloat16, jnp.float32
    qcols = slice(0, HEADS * HEAD)
    kcols = slice(HEADS * HEAD, (HEADS + 1) * HEAD)
    vcols = slice((HEADS + 1) * HEAD, (HEADS + 2) * HEAD)
    scale = 1.0 / math.sqrt(HEAD)
    low_q, low_k, low_v = (
        jnp.concatenate([low[b, n * RANK : (n + 1) * RANK] for b in range(BLOCKS)], axis=1)
        for n in range(KINDS)
    )
    keys[...] = (base[:, kcols].astype(f32) + matmul(low_k, up_half[:, kcols], TN)).astype(bf16)
    values[...] = (base[:, vcols].astype(f32) + matmul(low_v, up_half[:, vcols], TN)).astype(bf16)
    up_q = up_half[:, qcols]
    held, grads, next_dk, next_dv = {}, {}, {}, {}
    own_k, own_v = {}, {}

    def window(i):
        return slice(max(i - 1, 0) * BLOCK, (i + 1) * BLOCK)

    def stage_a(i):
        rows = slice(i * BLOCK, (i + 1) * BLOCK)
        q_wide = base[rows, qcols].astype(f32) + matmul(low[i, 0:RANK], up_q, TN)
        q_wide = q_wide.astype(bf16)
        q = jnp.concatenate([q_wide[:, h * HEAD : (h + 1) * HEAD] for h in range(HEADS)], axis=0)
        held[i] = q, matmul(keys[window(i)], q, NT)

    def stage_b(i):
        q, scores = held.pop(i)
        mask = masks[i] if i else masks[0, BLOCK:]
        mask = jnp.concatenate([mask] * HEADS, axis=1)
        scores = scores * (scale * math.log2(math.e)) + mask
        top = jnp.max(scores, axis=0, keepdims=True)
        weights = jnp.exp2(scores - top)
        total = jnp.sum(weights, axis=0, keepdims=True)
        probs = weights * (1.0 / total)
        prob_grad = matmul(values[window(i)], gs[i], NT)
        row_dot = jnp.sum(probs * prob_grad, axis=0, keepdims=True)
        score_grad = (probs * (prob_grad - row_dot)).astype(bf16)
        grads[i] = q, probs.astype(bf16), score_grad

    def stage_c(i):
        q, probs, score_grad = grads.pop(i)
        dk = matmul(score_grad, q)
        dv = matmul(probs, gs[i])
        key = keys[window(i)]
        dq = (matmul(key.astype(f32).T.astype(bf16), score_grad) * scale).astype(bf16)
        dq = jnp.concatenate(
            [dq[:, h * BLOCK : (h + 1) * BLOCK] for h in range(HEADS)], axis=0
        )
        dqs[:, i * BLOCK : (i + 1) * BLOCK] = dq
        dk_own, dv_own = dk[-BLOCK:], dv[-BLOCK:]
        if i < BLOCKS - 1:
            dk_own, dv_own = dk_own + next_dk.pop(i), dv_own + next_dv.pop(i)
        if i:
            next_dk[i - 1], next_dv[i - 1] = dk[:BLOCK], dv[:BLOCK]
        own_k[i], own_v[i] = (dk_own * scale).astype(bf16), dv_own.astype(bf16)
        plow[i, 0:RANK] = matmul(up_q, dq).astype(bf16)
        plow[i, RANK : 2 * RANK] = matmul(up_half[:, kcols], own_k[i], NT).astype(bf16)
        plow[i, 2 * RANK :] = matmul(up_half[:, vcols], own_v[i], NT).astype(bf16)
        done(i)

    stages = {"A": stage_a, "B": stage_b, "C": stage_c}
    for item in ORDER:
        stages[item[0]](int(item[1]))

    gup = matmul(low_q, dqs[...], NT) * 0.5
    gup_k = sum(matmul(low[b, RANK : 2 * RANK], own_k[b]) for b in range(BLOCKS)) * 0.5
    gup_v = sum(matmul(low[b, 2 * RANK :], own_v[b]) for b in range(BLOCKS)) * 0.5
    for j in range(CHIPS):
        upout[j, 0:RANK] = gup[:, j * HEAD : (j + 1) * HEAD].astype(bf16)
        upout[j, RANK:] = ((gup_v if j % 2 else gup_k) * mine(j // 2)).astype(bf16)


def fused_kernel(
    ids_hbm, x_hbm, base_hbm, grad_hbm, seg_hbm, down_hbm, up_hbm, out_a, out_b, out_u,
    ids, x_ref, base, grad, seg, down_ref, up_ref, masks, loads,
    part, inbox, low, s1, r1, s2, r2,
    up_half, keys, values, gs, dqs, plow, up_part, shared, s3, r3,
    down_early, down_a, down_b, in_a, in_b, in_u, sa, sb, su, ra, rb, ru,
    buf_a, buf_b, buf_u, *sems,
):
    bf16, f32 = jnp.bfloat16, jnp.float32
    chip, core = split_dp()
    tensor, dp = lax.axis_index("tensor"), lax.axis_index("dp")
    fetch = [
        pltpu.make_async_copy(src, dst, loads.at[n])
        for n, (src, dst) in enumerate(
            [
                (ids_hbm, ids), (down_hbm, down_ref), (x_hbm, x_ref), (up_hbm, up_ref),
                (grad_hbm, grad), (base_hbm, base), (seg_hbm, seg),
            ]
        )
    ]
    for copy in fetch:
        copy.start()

    barrier = pltpu.get_barrier_semaphore()
    greet_tensor(barrier)

    def greet(k, carry):
        other = (dp + k) % MEMBERS
        pl.semaphore_signal(barrier, inc=1, device_id=(other, tensor), device_id_type=MESH)
        return carry

    lax.fori_loop(1, MEMBERS, greet, 0)

    fetch[0].wait()
    adapter = ids[dp]
    fetch[1].wait()
    fetch[2].wait()
    partial_low = matmul(down_ref[adapter], x_ref[...], NT)
    for b in range(BLOCKS):
        part[b] = partial_low[:, b * BLOCK : (b + 1) * BLOCK].astype(bf16)
    pl.semaphore_wait(barrier, N_TENSOR - 1 + MEMBERS - 1)
    copies = tensor_scatter(part, inbox, s1, r1)
    fetch[3].wait()
    up_half[...] = (up_ref[adapter].astype(f32) * 0.5).astype(bf16)
    fetch[6].wait()
    fill_masks(seg, masks)
    fetch[4].wait()
    for b in range(BLOCKS):
        for h in range(HEADS):
            tile = grad[b * BLOCK : (b + 1) * BLOCK, h * HEAD : (h + 1) * HEAD]
            gs[b, h * BLOCK : (h + 1) * BLOCK] = tile
    fetch[5].wait()
    received(copies)
    tensor_reduce(inbox, low)
    more = tensor_gather(low, s2, r2)
    received(more)
    copies = copies + more

    shares = {}

    def done(i):
        shares[i] = share(plow.at[i], shared.at[i], s3.at[i], r3.at[i])

    def mine(a):
        return (adapter == a).astype(f32)

    attend(base, masks, low, up_half, keys, values, gs, dqs, plow, up_part, mine, done)
    scatter(up_part, in_u, 1, su, ru)

    def low_grad(b):
        received(shares[b])
        total = shared[b, 0].astype(f32)
        for n in range(1, N_TENSOR):
            total = total + shared[b, n].astype(f32)
        return total.astype(bf16)

    early = jnp.concatenate([low_grad(b) for b in range(1, BLOCKS)], axis=1)
    wide = N_Z * HEAD
    for s in range(N_Y):
        cols = slice(s * wide, (s + 1) * wide)
        down_early[:, cols] = matmul(early, x_ref[BLOCK:, cols])
    late = low_grad(0)
    y, z = chip // N_Z, chip % N_Z
    for s, dy in enumerate((2, 1, 3, 0)):
        there = (y + dy) % N_Y
        cols = pl.ds(pl.multiple_of(there * wide, wide), wide)
        product = (matmul(late, x_ref[:BLOCK, cols]) + down_early[:, cols]).astype(bf16)
        for j in range(N_Z):
            tile = product[:, j * HEAD : (j + 1) * HEAD]
            down_a[there * N_Z + j] = tile[: 2 * RANK]
            down_b[there * N_Z + j] = tile[2 * RANK :]
        for j in range(N_Z):
            if dy:
                p = there * N_Z + (1 - z // 2) * (3 - j) + (z // 2) * j
            else:
                p = there * N_Z + (z + j) % N_Z
            n = (4 + 4 * s + j) if dy else j
            if dy or j:
                piece(down_a, in_a, p, 0, sa.at[n], ra).start()
                piece(down_b, in_b, p, 1, sb.at[n], rb).start()
    own_piece(down_a, in_a, 0, sa, ra)
    own_piece(down_b, in_b, 1, sb, rb)

    stream_a = Stream(buf_a, out_a, 0, sems[0:7])
    stream_b = Stream(buf_b, out_b, 1, sems[7:14])
    stream_u = Stream(buf_u, out_u, 1, sems[14:21])

    @pl.when(core == 0)
    def _():
        arrived(in_a, ra)
        sum_adapters(ids, in_a, slice(0, 2 * RANK), buf_a, chip)
        stream_a.start()
        stream_a.spread()
        stream_a.finish()
        stream_a.sent()
        stream_b.receive()
        stream_u.receive()

    @pl.when(core == 1)
    def _():
        arrived(in_u, ru)
        sum_adapters(ids, in_u, slice(0, RANK), buf_u, chip)

        def one(m, total):
            return total + in_u[m, RANK:].astype(f32)

        total = lax.fori_loop(0, MEMBERS, one, jnp.zeros((RANK, HEAD), f32))
        buf_u[chip, ADAPTERS] = total.astype(bf16)
        stream_u.start()
        arrived(in_b, rb)
        sum_adapters(ids, in_b, slice(0, RANK), buf_b, chip)
        stream_b.start()
        stream_u.spread()
        stream_b.spread()
        stream_u.finish()
        stream_b.finish()
        stream_u.sent()
        stream_b.sent()
        stream_a.receive()

    sent(copies + sum(shares.values(), []))
    scatter_sent(up_part, in_u, 1, su, ru)
    scatter_sent(down_a, in_a, 0, sa, ra)
    scatter_sent(down_b, in_b, 1, sb, rb)


def widen_kernel(a_ref, b_ref, u_ref, down_hbm, up_hbm, down, up, sems):
    stores = []
    for a in range(ADAPTERS):
        for j in range(CHIPS):
            cols = slice(j * HEAD, (j + 1) * HEAD)
            down[a, : 2 * RANK, cols] = a_ref[j, a].astype(jnp.float32)
            down[a, 2 * RANK :, cols] = b_ref[j, a].astype(jnp.float32)
            up[a, :, cols] = u_ref[j, a].astype(jnp.float32)
        for kind in range(2):
            cols = slice((CHIPS + kind) * HEAD, (CHIPS + kind + 1) * HEAD)
            up[a, :, cols] = u_ref[2 * a + kind, ADAPTERS].astype(jnp.float32)
        for n, (src, dst) in enumerate([(down, down_hbm), (up, up_hbm)]):
            stores.append(pltpu.make_async_copy(src.at[a], dst.at[a], sems.at[n, a]))
            stores[-1].start()
    for copy in stores:
        copy.wait()


def hbm():
    return pl.BlockSpec(memory_space=pl.ANY)


def per_device(x, base, grad, segments, ids, down, up):
    bf16, f32 = jnp.bfloat16, jnp.float32
    ids = ids.reshape(-1)
    x, base, grad, segments, ids, down, up = (
        pltpu.with_memory_space_constraint(v, pltpu.HBM)
        for v in (x, base, grad, segments, ids, down, up)
    )
    tokens, width = x.shape
    cols = base.shape[1]
    rows = KINDS * RANK
    limit = 40 * 1024 * 1024
    out_a, out_b, out_u = pl.pallas_call(
        fused_kernel,
        out_shape=(
            jax.ShapeDtypeStruct((CHIPS, ADAPTERS, 2 * RANK, HEAD), bf16),
            jax.ShapeDtypeStruct((CHIPS, ADAPTERS, RANK, HEAD), bf16),
            jax.ShapeDtypeStruct((CHIPS, ADAPTERS + 1, RANK, HEAD), bf16),
        ),
        in_specs=[hbm()] * 7,
        out_specs=(hbm(), hbm(), hbm()),
        scratch_shapes=[
            SMEM((MEMBERS,), jnp.int32),
            VMEM(x.shape, bf16), VMEM(base.shape, bf16), VMEM(grad.shape, bf16),
            VMEM(segments.shape, jnp.int32),
            VMEM(down.shape, bf16), VMEM(up.shape, bf16),
            VMEM((BLOCKS, 2 * BLOCK, BLOCK), f32), DMA((7,)),
            VMEM((BLOCKS, rows, BLOCK), bf16),
            VMEM((N_TENSOR, rows, BLOCK), bf16),
            VMEM((BLOCKS, rows, BLOCK), bf16),
            DMA((7,)), DMA((7,)), DMA((3,)), DMA((3,)),
            VMEM((RANK, cols), bf16),
            VMEM((tokens, HEAD), bf16),
            VMEM((tokens, HEAD), bf16),
            VMEM((BLOCKS, HEADS * BLOCK, HEAD), bf16),
            VMEM((HEADS * HEAD, tokens), bf16),
            VMEM((BLOCKS, rows, BLOCK), bf16),
            VMEM((CHIPS, 2 * RANK, HEAD), bf16),
            VMEM((BLOCKS, N_TENSOR, rows, BLOCK), bf16),
            DMA((BLOCKS, 7)), DMA((BLOCKS, 7)),
            VMEM((rows, width), f32),
            VMEM((CHIPS, 2 * RANK, HEAD), bf16),
            VMEM((CHIPS, RANK, HEAD), bf16),
            VMEM((MEMBERS, 2 * RANK, HEAD), bf16),
            VMEM((MEMBERS, RANK, HEAD), bf16),
            VMEM((MEMBERS, 2 * RANK, HEAD), bf16),
            DMA((CHIPS,)), DMA((CHIPS,)), DMA((CHIPS,)),
            DMA, DMA, DMA,
            VMEM((CHIPS, ADAPTERS, 2 * RANK, HEAD), bf16),
            VMEM((CHIPS, ADAPTERS, RANK, HEAD), bf16),
            VMEM((CHIPS, ADAPTERS + 1, RANK, HEAD), bf16),
        ] + STREAM_SEMS * 3,
        compiler_params=pltpu.CompilerParams(
            collective_id=0, has_side_effects=True, vmem_limit_bytes=limit
        ),
        name="fused",
    )(ids, x, base, grad, segments, down, up)

    return pl.pallas_call(
        widen_kernel,
        out_shape=(
            jax.ShapeDtypeStruct((ADAPTERS, rows, width), f32),
            jax.ShapeDtypeStruct((ADAPTERS, RANK, cols), f32),
        ),
        in_specs=[vmem()] * 3,
        out_specs=(hbm(), hbm()),
        scratch_shapes=[
            VMEM((ADAPTERS, rows, width), f32),
            VMEM((ADAPTERS, RANK, cols), f32),
            DMA((2, ADAPTERS)),
        ],
        compiler_params=pltpu.CompilerParams(vmem_limit_bytes=limit),
        name="widen",
    )(out_a, out_b, out_u)


def solution(mesh):
    placed = (
        P("dp", "tensor"),
        P("dp", "tensor"),
        P("dp", "tensor"),
        P("dp", None),
        P(),
        P(None, None, "tensor"),
        P(None, None, "tensor"),
    )
    return jax.shard_map(
        per_device,
        mesh=mesh,
        in_specs=placed,
        out_specs=(P(None, None, "tensor"), P(None, None, "tensor")),
        check_vma=False,
    )
```

```python
import functools
import math

import jax
import jax.numpy as jnp
from jax import lax
from jax.experimental import pallas as pl
from jax.experimental.pallas import tpu as pltpu
from jax.sharding import PartitionSpec as P

MESH = pl.DeviceIdType.MESH
VMEM = pltpu.VMEM
SMEM = pltpu.SMEM
DMA = pltpu.SemaphoreType.DMA

HEAD = 128
RANK = 16
HEADS = 16
KINDS = 3
BLOCK = 128
N_TENSOR = 8
N_X = 4
N_Y = 4
N_Z = 4
CHIPS = N_Y * N_Z
MEMBERS = 2 * CHIPS
ADAPTERS = 8
BLOCKS = 4
masked_score = -1e30

NT = (((1,), (1,)), ((), ()))
TN = (((0,), (0,)), ((), ()))
NN = (((1,), (0,)), ((), ()))


def matmul(a, b, dims=NN):
    return lax.dot_general(a, b, dims, preferred_element_type=jnp.float32)


def vmem():
    return pl.BlockSpec(memory_space=VMEM)


def smem():
    return pl.BlockSpec(memory_space=SMEM)


FAR_FIRST = ((1, 2), (1, 1), (1, 3), (1, 0), (0, 2), (0, 1), (0, 3))


def tensor_peers():
    me = lax.axis_index("tensor")
    x, high = me % N_X, me // N_X
    return [((high + dh) % 2) * N_X + (x + dx) % N_X for dh, dx in FAR_FIRST]


def greet_tensor(barrier):
    dp = lax.axis_index("dp")
    for other in tensor_peers():
        pl.semaphore_signal(barrier, inc=1, device_id=(dp, other), device_id_type=MESH)


def tensor_scatter(part, inbox, send, recv):
    dp, me = lax.axis_index("dp"), lax.axis_index("tensor")
    copies = []
    for n, other in enumerate(tensor_peers()):
        copies.append(
            pltpu.make_async_remote_copy(
                src_ref=part.at[other % N_X],
                dst_ref=inbox.at[me],
                send_sem=send.at[n],
                recv_sem=recv.at[n],
                device_id=(dp, other),
                device_id_type=MESH,
            )
        )
        copies[-1].start()
    inbox[me] = part[me % N_X]
    return copies


def tensor_reduce(inbox, full):
    me = lax.axis_index("tensor")
    total = inbox[0].astype(jnp.float32)
    for i in range(1, N_TENSOR):
        total = total + inbox[i].astype(jnp.float32)
    full[me % N_X] = total.astype(jnp.bfloat16)


def tensor_gather(full, send, recv):
    dp, me = lax.axis_index("dp"), lax.axis_index("tensor")
    x, high = me % N_X, me // N_X
    copies = []
    for d in range(1, N_X):
        other = high * N_X + (x + d) % N_X
        copies.append(
            pltpu.make_async_remote_copy(
                src_ref=full.at[x],
                dst_ref=full.at[x],
                send_sem=send.at[d - 1],
                recv_sem=recv.at[d - 1],
                device_id=(dp, other),
                device_id_type=MESH,
            )
        )
        copies[-1].start()
    return copies


def received(copies):
    for copy in copies:
        copy.wait_recv()


def sent(copies):
    for copy in copies:
        copy.wait_send()


def split_dp():
    dp = lax.axis_index("dp")
    return dp // 2, dp % 2


def piece(src, inbox, p, core_to, send, recv):
    dp, tensor = lax.axis_index("dp"), lax.axis_index("tensor")
    return pltpu.make_async_remote_copy(
        src_ref=src.at[p],
        dst_ref=inbox.at[dp],
        send_sem=send,
        recv_sem=recv,
        device_id=(2 * p + core_to, tensor),
        device_id_type=MESH,
    )


def own_piece(src, inbox, core_to, send, recv):
    chip, core = split_dp()

    @pl.when(core == core_to)
    def _():
        pltpu.make_async_copy(src.at[chip], inbox.at[lax.axis_index("dp")], recv).start()

    @pl.when(core != core_to)
    def _():
        piece(src, inbox, chip, core_to, send.at[0], recv).start()


def scatter(src, inbox, core_to, send, recv):
    chip, _ = split_dp()

    def one(k, carry):
        piece(src, inbox, (chip + k) % CHIPS, core_to, send.at[k], recv).start()
        return carry

    lax.fori_loop(1, CHIPS, one, 0)
    own_piece(src, inbox, core_to, send, recv)


def scatter_sent(src, inbox, core_to, send, recv):
    chip, core = split_dp()

    def one(k, carry):
        piece(src, inbox, chip, core_to, send.at[k], recv).wait_send()
        return carry

    lax.fori_loop(1, CHIPS, one, 0)

    @pl.when(core != core_to)
    def _():
        one(0, 0)


def arrived(whole, sem):
    pltpu.make_async_copy(whole, whole, sem).wait()


def sum_adapters(ids, inbox, rows, out, slot):
    def one(m, sums):
        term = inbox[m, rows].astype(jnp.float32)
        adapter = ids[m]
        return tuple(
            sums[a] + term * (adapter == a).astype(jnp.float32) for a in range(ADAPTERS)
        )

    zero = jnp.zeros((rows.stop - rows.start, HEAD), jnp.float32)
    sums = lax.fori_loop(0, MEMBERS, one, (zero,) * ADAPTERS)
    for a in range(ADAPTERS):
        out[slot, a] = sums[a].astype(jnp.bfloat16)


class Stream:
    def __init__(self, buf, out, owner, sems):
        self.buf, self.out, self.owner = buf, out, owner
        self.zs, self.zr, self.ys, self.yr, self.fs, self.fr, self.cs, self.cr, self.ks = sems
        self.half = buf.shape[1] // 2
        self.tensor = lax.axis_index("tensor")
        self.chip, self.core = split_dp()
        self.y, self.z = self.chip // N_Z, self.chip % N_Z

    def copy(self, slot, chip_to, core_to, send, recv, dst=None):
        return pltpu.make_async_remote_copy(
            src_ref=self.buf.at[slot],
            dst_ref=(self.buf if dst is None else dst).at[slot],
            send_sem=send,
            recv_sem=recv,
            device_id=(2 * chip_to + core_to, self.tensor),
            device_id_type=MESH,
        )

    def at(self, dy, dz):
        return ((self.y + dy + N_Y) % N_Y) * N_Z + (self.z + dz + N_Z) % N_Z

    def nearest_first(self):
        z, high = self.z, self.z // 2
        sources = (z + 1 - 2 * (z % 2), 2 - high, 3 * (1 - high))
        return [(z - source + N_Z) % N_Z for source in sources]

    def z_copy(self, d):
        return self.copy(
            self.chip, self.at(0, d), self.owner, self.zs.at[d - 1], self.zr.at[d - 1]
        )

    def y_copy(self, dz, dy):
        n = 3 * dz + dy - 1
        return self.copy(self.at(0, -dz), self.at(dy, 0), self.owner, self.ys.at[n], self.yr.at[n])

    def twin(self, n, slot):
        return self.copy(
            slot, self.chip, 1 - self.owner, self.cs.at[n], self.cr, self.out
        )

    def deliver(self, n, slot):
        self.twin(n, slot).start()
        pltpu.make_async_copy(self.buf.at[slot], self.out.at[slot], self.ks).start()

    def y_sends(self, dz, steps=(2, 1, 3)):
        for dy in steps:
            self.y_copy(dz, dy).start()
        self.deliver(dz, self.at(0, -dz))

    def forward(self, k, dz, side):
        part = pl.ds(0, self.half) if side == 0 else pl.ds(self.half, self.buf.shape[1] - self.half)
        slot, to = self.at(2 * side - 1, -dz), self.at(1 - 2 * side, 0)
        return self.forward_copy(k, slot, to, side, part)

    def forwarded(self, k, dz, side):
        part = pl.ds(0, self.half) if side == 0 else pl.ds(self.half, self.buf.shape[1] - self.half)
        return self.forward_copy(k, self.at(2, -dz), self.chip, side, part)

    def forward_copy(self, k, slot, to, side, part):
        return pltpu.make_async_remote_copy(
            src_ref=self.buf.at[slot, part],
            dst_ref=self.buf.at[slot, part],
            send_sem=self.fs.at[2 * k + side],
            recv_sem=self.fr.at[2 * k + side],
            device_id=(2 * to + self.owner, self.tensor),
            device_id_type=MESH,
        )

    def start(self):
        for d in (2, 1, 3):
            self.z_copy(d).start()
        self.y_sends(0, (1, 3))

    def pass_on(self, k, dz):
        for side, dy in enumerate((1, 3)):
            self.y_copy(dz, dy).wait_recv()
            self.forward(k, dz, side).start()
            self.deliver(4 + 3 * dz + dy - 1, self.at(-dy, -dz))

    def spread(self):
        near, middle, far = self.nearest_first()
        self.z_copy(near).wait_recv()
        self.y_sends(near, (1, 3))
        self.z_copy(middle).wait_recv()
        self.y_sends(middle)
        self.pass_on(0, 0)
        self.z_copy(far).wait_recv()
        self.y_sends(far)
        self.pass_on(1, near)

    def finish(self):
        near, middle, far = self.nearest_first()
        for dz in (middle, far):
            for dy in (1, 3, 2):
                self.y_copy(dz, dy).wait_recv()
                self.deliver(4 + 3 * dz + dy - 1, self.at(-dy, -dz))
            k, other = (0, 0) if dz is middle else (1, near)
            for side in range(2):
                self.forwarded(k, other, side).wait_recv()
            self.deliver(4 + 3 * other + 1, self.at(2, -other))

    def sent(self):
        near, middle, far = self.nearest_first()
        for d in range(1, N_Z):
            self.z_copy(d).wait_send()
        for dz, steps in ((0, (1, 3)), (near, (1, 3)), (middle, (1, 2, 3)), (far, (1, 2, 3))):
            for dy in steps:
                self.y_copy(dz, dy).wait_send()
        for k, dz in enumerate((0, near)):
            for side in range(2):
                self.forward(k, dz, side).wait_send()
        for n in range(CHIPS):
            self.twin(n, self.chip).wait_send()
        pltpu.make_async_copy(self.buf, self.out, self.ks).wait()

    def receive(self):
        arrived(self.out, self.cr)


STREAM_SEMS = [DMA((3,))] * 2 + [DMA((12,))] * 2 + [DMA((4,))] * 2 + [DMA((CHIPS,)), DMA, DMA]


def share(part, inbox, send, recv):
    dp, me = lax.axis_index("dp"), lax.axis_index("tensor")
    copies = []
    for n, other in enumerate(tensor_peers()):
        copies.append(
            pltpu.make_async_remote_copy(
                src_ref=part,
                dst_ref=inbox.at[me],
                send_sem=send.at[n],
                recv_sem=recv.at[n],
                device_id=(dp, other),
                device_id_type=MESH,
            )
        )
        copies[-1].start()
    inbox[me] = part[...]
    return copies


def fill_masks(seg, masks):
    u = lax.broadcasted_iota(jnp.int32, (BLOCK, BLOCK), 0)
    t = lax.broadcasted_iota(jnp.int32, (BLOCK, BLOCK), 1)
    docs = [
        jnp.broadcast_to(
            seg[:, b * BLOCK : (b + 1) * BLOCK].astype(jnp.float32), (BLOCK, BLOCK)
        )
        for b in range(BLOCKS)
    ]
    for i in range(BLOCKS):
        masks[i, BLOCK:] = jnp.where((docs[i].T == docs[i]) & (u <= t), 0.0, masked_score)
        if i:
            masks[i, :BLOCK] = jnp.where(docs[i - 1].T == docs[i], 0.0, masked_score)


ORDER = "A3 B3 A2 C3 B2 A1 C2 B1 A0 C1 B0 C0".split()


def attend(base, masks, low, up_half, keys, values, gs, dqs, plow, upout, mine, done):
    bf16, f32 = jnp.bfloat16, jnp.float32
    qcols = slice(0, HEADS * HEAD)
    kcols = slice(HEADS * HEAD, (HEADS + 1) * HEAD)
    vcols = slice((HEADS + 1) * HEAD, (HEADS + 2) * HEAD)
    scale = 1.0 / math.sqrt(HEAD)
    low_q, low_k, low_v = (
        jnp.concatenate([low[b, n * RANK : (n + 1) * RANK] for b in range(BLOCKS)], axis=1)
        for n in range(KINDS)
    )
    keys[...] = (base[:, kcols].astype(f32) + matmul(low_k, up_half[:, kcols], TN)).astype(bf16)
    values[...] = (base[:, vcols].astype(f32) + matmul(low_v, up_half[:, vcols], TN)).astype(bf16)
    up_q = up_half[:, qcols]
    held, grads, next_dk, next_dv = {}, {}, {}, {}
    own_k, own_v = {}, {}

    def window(i):
        return slice(max(i - 1, 0) * BLOCK, (i + 1) * BLOCK)

    def stage_a(i):
        rows = slice(i * BLOCK, (i + 1) * BLOCK)
        q_wide = base[rows, qcols].astype(f32) + matmul(low[i, 0:RANK], up_q, TN)
        q_wide = q_wide.astype(bf16)
        q = jnp.concatenate([q_wide[:, h * HEAD : (h + 1) * HEAD] for h in range(HEADS)], axis=0)
        held[i] = q, matmul(keys[window(i)], q, NT)

    def stage_b(i):
        q, scores = held.pop(i)
        mask = masks[i] if i else masks[0, BLOCK:]
        mask = jnp.concatenate([mask] * HEADS, axis=1)
        scores = scores * (scale * math.log2(math.e)) + mask
        top = jnp.max(scores, axis=0, keepdims=True)
        weights = jnp.exp2(scores - top)
        total = jnp.sum(weights, axis=0, keepdims=True)
        probs = weights * (1.0 / total)
        prob_grad = matmul(values[window(i)], gs[i], NT)
        row_dot = jnp.sum(probs * prob_grad, axis=0, keepdims=True)
        score_grad = (probs * (prob_grad - row_dot)).astype(bf16)
        grads[i] = q, probs.astype(bf16), score_grad

    def stage_c(i):
        q, probs, score_grad = grads.pop(i)
        dk = matmul(score_grad, q)
        dv = matmul(probs, gs[i])
        key = keys[window(i)]
        dq = (matmul(key.astype(f32).T.astype(bf16), score_grad) * scale).astype(bf16)
        dq = jnp.concatenate(
            [dq[:, h * BLOCK : (h + 1) * BLOCK] for h in range(HEADS)], axis=0
        )
        dqs[:, i * BLOCK : (i + 1) * BLOCK] = dq
        dk_own, dv_own = dk[-BLOCK:], dv[-BLOCK:]
        if i < BLOCKS - 1:
            dk_own, dv_own = dk_own + next_dk.pop(i), dv_own + next_dv.pop(i)
        if i:
            next_dk[i - 1], next_dv[i - 1] = dk[:BLOCK], dv[:BLOCK]
        own_k[i], own_v[i] = (dk_own * scale).astype(bf16), dv_own.astype(bf16)
        plow[i, 0:RANK] = matmul(up_q, dq).astype(bf16)
        plow[i, RANK : 2 * RANK] = matmul(up_half[:, kcols], own_k[i], NT).astype(bf16)
        plow[i, 2 * RANK :] = matmul(up_half[:, vcols], own_v[i], NT).astype(bf16)
        done(i)

    stages = {"A": stage_a, "B": stage_b, "C": stage_c}
    for item in ORDER:
        stages[item[0]](int(item[1]))

    gup = matmul(low_q, dqs[...], NT) * 0.5
    gup_k = sum(matmul(low[b, RANK : 2 * RANK], own_k[b]) for b in range(BLOCKS)) * 0.5
    gup_v = sum(matmul(low[b, 2 * RANK :], own_v[b]) for b in range(BLOCKS)) * 0.5
    for j in range(CHIPS):
        upout[j, 0:RANK] = gup[:, j * HEAD : (j + 1) * HEAD].astype(bf16)
        upout[j, RANK:] = ((gup_v if j % 2 else gup_k) * mine(j // 2)).astype(bf16)


def fused_kernel(
    ids_hbm, x_hbm, base_hbm, grad_hbm, seg_hbm, down_hbm, up_hbm, out_a, out_b, out_u,
    ids, x_ref, base, grad, seg, down_ref, up_ref, masks, loads,
    part, inbox, low, s1, r1, s2, r2,
    up_half, keys, values, gs, dqs, plow, up_part, shared, s3, r3,
    down_early, down_a, down_b, in_a, in_b, in_u, sa, sb, su, ra, rb, ru,
    buf_a, buf_b, buf_u, *sems,
):
    bf16, f32 = jnp.bfloat16, jnp.float32
    chip, core = split_dp()
    tensor, dp = lax.axis_index("tensor"), lax.axis_index("dp")
    fetch = [
        pltpu.make_async_copy(src, dst, loads.at[n])
        for n, (src, dst) in enumerate(
            [
                (ids_hbm, ids), (down_hbm, down_ref), (x_hbm, x_ref), (up_hbm, up_ref),
                (grad_hbm, grad), (base_hbm, base), (seg_hbm, seg),
            ]
        )
    ]
    for copy in fetch:
        copy.start()

    barrier = pltpu.get_barrier_semaphore()
    greet_tensor(barrier)

    def greet(k, carry):
        other = (dp + k) % MEMBERS
        pl.semaphore_signal(barrier, inc=1, device_id=(other, tensor), device_id_type=MESH)
        return carry

    lax.fori_loop(1, MEMBERS, greet, 0)

    fetch[0].wait()
    adapter = ids[dp]
    fetch[1].wait()
    fetch[2].wait()
    partial_low = matmul(down_ref[adapter], x_ref[...], NT)
    for b in range(BLOCKS):
        part[b] = partial_low[:, b * BLOCK : (b + 1) * BLOCK].astype(bf16)
    pl.semaphore_wait(barrier, N_TENSOR - 1 + MEMBERS - 1)
    copies = tensor_scatter(part, inbox, s1, r1)
    fetch[3].wait()
    up_half[...] = (up_ref[adapter].astype(f32) * 0.5).astype(bf16)
    fetch[6].wait()
    fill_masks(seg, masks)
    fetch[4].wait()
    for b in range(BLOCKS):
        for h in range(HEADS):
            tile = grad[b * BLOCK : (b + 1) * BLOCK, h * HEAD : (h + 1) * HEAD]
            gs[b, h * BLOCK : (h + 1) * BLOCK] = tile
    fetch[5].wait()
    received(copies)
    tensor_reduce(inbox, low)
    more = tensor_gather(low, s2, r2)
    received(more)
    copies = copies + more

    shares = {}

    def done(i):
        shares[i] = share(plow.at[i], shared.at[i], s3.at[i], r3.at[i])

    def mine(a):
        return (adapter == a).astype(f32)

    attend(base, masks, low, up_half, keys, values, gs, dqs, plow, up_part, mine, done)
    scatter(up_part, in_u, 1, su, ru)

    def low_grad(b):
        received(shares[b])
        total = shared[b, 0].astype(f32)
        for n in range(1, N_TENSOR):
            total = total + shared[b, n].astype(f32)
        return total.astype(bf16)

    early = jnp.concatenate([low_grad(b) for b in range(1, BLOCKS)], axis=1)
    wide = N_Z * HEAD
    for s in range(N_Y):
        cols = slice(s * wide, (s + 1) * wide)
        down_early[:, cols] = matmul(early, x_ref[BLOCK:, cols])
    late = low_grad(0)
    y, z = chip // N_Z, chip % N_Z
    for s, dy in enumerate((2, 1, 3, 0)):
        there = (y + dy) % N_Y
        cols = pl.ds(pl.multiple_of(there * wide, wide), wide)
        product = (matmul(late, x_ref[:BLOCK, cols]) + down_early[:, cols]).astype(bf16)
        for j in range(N_Z):
            tile = product[:, j * HEAD : (j + 1) * HEAD]
            down_a[there * N_Z + j] = tile[: 2 * RANK]
            down_b[there * N_Z + j] = tile[2 * RANK :]
        for j in range(N_Z):
            if dy:
                p = there * N_Z + (1 - z // 2) * (3 - j) + (z // 2) * j
            else:
                p = there * N_Z + (z + j) % N_Z
            n = (4 + 4 * s + j) if dy else j
            if dy or j:
                piece(down_a, in_a, p, 0, sa.at[n], ra).start()
                piece(down_b, in_b, p, 1, sb.at[n], rb).start()
    own_piece(down_a, in_a, 0, sa, ra)
    own_piece(down_b, in_b, 1, sb, rb)

    stream_a = Stream(buf_a, out_a, 0, sems[0:9])
    stream_b = Stream(buf_b, out_b, 1, sems[9:18])
    stream_u = Stream(buf_u, out_u, 1, sems[18:27])

    @pl.when(core == 0)
    def _():
        arrived(in_a, ra)
        sum_adapters(ids, in_a, slice(0, 2 * RANK), buf_a, chip)
        stream_a.start()
        stream_a.spread()
        stream_a.finish()
        stream_a.sent()
        stream_b.receive()
        stream_u.receive()

    @pl.when(core == 1)
    def _():
        arrived(in_u, ru)
        sum_adapters(ids, in_u, slice(0, RANK), buf_u, chip)

        def one(m, total):
            return total + in_u[m, RANK:].astype(f32)

        total = lax.fori_loop(0, MEMBERS, one, jnp.zeros((RANK, HEAD), f32))
        buf_u[chip, ADAPTERS] = total.astype(bf16)
        stream_u.start()
        arrived(in_b, rb)
        sum_adapters(ids, in_b, slice(0, RANK), buf_b, chip)
        stream_b.start()
        stream_u.spread()
        stream_b.spread()
        stream_u.finish()
        stream_b.finish()
        stream_u.sent()
        stream_b.sent()
        stream_a.receive()

    sent(copies + sum(shares.values(), []))
    scatter_sent(up_part, in_u, 1, su, ru)
    scatter_sent(down_a, in_a, 0, sa, ra)
    scatter_sent(down_b, in_b, 1, sb, rb)


def widen_kernel(a_ref, b_ref, u_ref, down_hbm, up_hbm, down, up, sems):
    stores = []
    for a in range(ADAPTERS):
        for j in range(CHIPS):
            cols = slice(j * HEAD, (j + 1) * HEAD)
            down[a, : 2 * RANK, cols] = a_ref[j, a].astype(jnp.float32)
            down[a, 2 * RANK :, cols] = b_ref[j, a].astype(jnp.float32)
            up[a, :, cols] = u_ref[j, a].astype(jnp.float32)
        for kind in range(2):
            cols = slice((CHIPS + kind) * HEAD, (CHIPS + kind + 1) * HEAD)
            up[a, :, cols] = u_ref[2 * a + kind, ADAPTERS].astype(jnp.float32)
        for n, (src, dst) in enumerate([(down, down_hbm), (up, up_hbm)]):
            stores.append(pltpu.make_async_copy(src.at[a], dst.at[a], sems.at[n, a]))
            stores[-1].start()
    for copy in stores:
        copy.wait()


def hbm():
    return pl.BlockSpec(memory_space=pl.ANY)


def per_device(x, base, grad, segments, ids, down, up):
    bf16, f32 = jnp.bfloat16, jnp.float32
    ids = ids.reshape(-1)
    x, base, grad, segments, ids, down, up = (
        pltpu.with_memory_space_constraint(v, pltpu.HBM)
        for v in (x, base, grad, segments, ids, down, up)
    )
    tokens, width = x.shape
    cols = base.shape[1]
    rows = KINDS * RANK
    limit = 40 * 1024 * 1024
    out_a, out_b, out_u = pl.pallas_call(
        fused_kernel,
        out_shape=(
            jax.ShapeDtypeStruct((CHIPS, ADAPTERS, 2 * RANK, HEAD), bf16),
            jax.ShapeDtypeStruct((CHIPS, ADAPTERS, RANK, HEAD), bf16),
            jax.ShapeDtypeStruct((CHIPS, ADAPTERS + 1, RANK, HEAD), bf16),
        ),
        in_specs=[hbm()] * 7,
        out_specs=(hbm(), hbm(), hbm()),
        scratch_shapes=[
            SMEM((MEMBERS,), jnp.int32),
            VMEM(x.shape, bf16), VMEM(base.shape, bf16), VMEM(grad.shape, bf16),
            VMEM(segments.shape, jnp.int32),
            VMEM(down.shape, bf16), VMEM(up.shape, bf16),
            VMEM((BLOCKS, 2 * BLOCK, BLOCK), f32), DMA((7,)),
            VMEM((BLOCKS, rows, BLOCK), bf16),
            VMEM((N_TENSOR, rows, BLOCK), bf16),
            VMEM((BLOCKS, rows, BLOCK), bf16),
            DMA((7,)), DMA((7,)), DMA((3,)), DMA((3,)),
            VMEM((RANK, cols), bf16),
            VMEM((tokens, HEAD), bf16),
            VMEM((tokens, HEAD), bf16),
            VMEM((BLOCKS, HEADS * BLOCK, HEAD), bf16),
            VMEM((HEADS * HEAD, tokens), bf16),
            VMEM((BLOCKS, rows, BLOCK), bf16),
            VMEM((CHIPS, 2 * RANK, HEAD), bf16),
            VMEM((BLOCKS, N_TENSOR, rows, BLOCK), bf16),
            DMA((BLOCKS, 7)), DMA((BLOCKS, 7)),
            VMEM((rows, width), f32),
            VMEM((CHIPS, 2 * RANK, HEAD), bf16),
            VMEM((CHIPS, RANK, HEAD), bf16),
            VMEM((MEMBERS, 2 * RANK, HEAD), bf16),
            VMEM((MEMBERS, RANK, HEAD), bf16),
            VMEM((MEMBERS, 2 * RANK, HEAD), bf16),
            DMA((CHIPS,)), DMA((CHIPS,)), DMA((CHIPS,)),
            DMA, DMA, DMA,
            VMEM((CHIPS, ADAPTERS, 2 * RANK, HEAD), bf16),
            VMEM((CHIPS, ADAPTERS, RANK, HEAD), bf16),
            VMEM((CHIPS, ADAPTERS + 1, RANK, HEAD), bf16),
        ] + STREAM_SEMS * 3,
        compiler_params=pltpu.CompilerParams(
            collective_id=0, has_side_effects=True, vmem_limit_bytes=limit
        ),
        name="fused",
    )(ids, x, base, grad, segments, down, up)

    return pl.pallas_call(
        widen_kernel,
        out_shape=(
            jax.ShapeDtypeStruct((ADAPTERS, rows, width), f32),
            jax.ShapeDtypeStruct((ADAPTERS, RANK, cols), f32),
        ),
        in_specs=[vmem()] * 3,
        out_specs=(hbm(), hbm()),
        scratch_shapes=[
            VMEM((ADAPTERS, rows, width), f32),
            VMEM((ADAPTERS, RANK, cols), f32),
            DMA((2, ADAPTERS)),
        ],
        compiler_params=pltpu.CompilerParams(vmem_limit_bytes=limit),
        name="widen",
    )(out_a, out_b, out_u)


def solution(mesh):
    placed = (
        P("dp", "tensor"),
        P("dp", "tensor"),
        P("dp", "tensor"),
        P("dp", None),
        P(),
        P(None, None, "tensor"),
        P(None, None, "tensor"),
    )
    return jax.shard_map(
        per_device,
        mesh=mesh,
        in_specs=placed,
        out_specs=(P(None, None, "tensor"), P(None, None, "tensor")),
        check_vma=False,
    )
```

```python
import functools
import math

import jax
import jax.numpy as jnp
from jax import lax
from jax.experimental import pallas as pl
from jax.experimental.pallas import tpu as pltpu
from jax.sharding import PartitionSpec as P

MESH = pl.DeviceIdType.MESH
VMEM = pltpu.VMEM
SMEM = pltpu.SMEM
DMA = pltpu.SemaphoreType.DMA

HEAD = 128
RANK = 16
HEADS = 16
KINDS = 3
BLOCK = 128
N_TENSOR = 8
N_X = 4
N_Y = 4
N_Z = 4
CHIPS = N_Y * N_Z
MEMBERS = 2 * CHIPS
ADAPTERS = 8
BLOCKS = 4
masked_score = -1e30

NT = (((1,), (1,)), ((), ()))
TN = (((0,), (0,)), ((), ()))
NN = (((1,), (0,)), ((), ()))


def matmul(a, b, dims=NN):
    return lax.dot_general(a, b, dims, preferred_element_type=jnp.float32)


def vmem():
    return pl.BlockSpec(memory_space=VMEM)


def smem():
    return pl.BlockSpec(memory_space=SMEM)


FAR_FIRST = ((1, 2), (1, 1), (1, 3), (1, 0), (0, 2), (0, 1), (0, 3))


def tensor_peers():
    me = lax.axis_index("tensor")
    x, high = me % N_X, me // N_X
    return [((high + dh) % 2) * N_X + (x + dx) % N_X for dh, dx in FAR_FIRST]


def greet_tensor(barrier):
    dp = lax.axis_index("dp")
    for other in tensor_peers():
        pl.semaphore_signal(barrier, inc=1, device_id=(dp, other), device_id_type=MESH)


def tensor_scatter(part, inbox, send, recv):
    dp, me = lax.axis_index("dp"), lax.axis_index("tensor")
    copies = []
    for n, other in enumerate(tensor_peers()):
        copies.append(
            pltpu.make_async_remote_copy(
                src_ref=part.at[other % N_X],
                dst_ref=inbox.at[me],
                send_sem=send.at[n],
                recv_sem=recv.at[n],
                device_id=(dp, other),
                device_id_type=MESH,
            )
        )
        copies[-1].start()
    inbox[me] = part[me % N_X]
    return copies


def tensor_reduce(inbox, full):
    me = lax.axis_index("tensor")
    total = inbox[0].astype(jnp.float32)
    for i in range(1, N_TENSOR):
        total = total + inbox[i].astype(jnp.float32)
    full[me % N_X] = total.astype(jnp.bfloat16)


def tensor_gather(full, send, recv):
    dp, me = lax.axis_index("dp"), lax.axis_index("tensor")
    x, high = me % N_X, me // N_X
    copies = []
    for d in range(1, N_X):
        other = high * N_X + (x + d) % N_X
        copies.append(
            pltpu.make_async_remote_copy(
                src_ref=full.at[x],
                dst_ref=full.at[x],
                send_sem=send.at[d - 1],
                recv_sem=recv.at[d - 1],
                device_id=(dp, other),
                device_id_type=MESH,
            )
        )
        copies[-1].start()
    return copies


def received(copies):
    for copy in copies:
        copy.wait_recv()


def sent(copies):
    for copy in copies:
        copy.wait_send()


def split_dp():
    dp = lax.axis_index("dp")
    return dp // 2, dp % 2


def piece(src, inbox, p, core_to, send, recv):
    dp, tensor = lax.axis_index("dp"), lax.axis_index("tensor")
    return pltpu.make_async_remote_copy(
        src_ref=src.at[p],
        dst_ref=inbox.at[dp],
        send_sem=send,
        recv_sem=recv,
        device_id=(2 * p + core_to, tensor),
        device_id_type=MESH,
    )


def own_piece(src, inbox, core_to, send, recv):
    chip, core = split_dp()

    @pl.when(core == core_to)
    def _():
        pltpu.make_async_copy(src.at[chip], inbox.at[lax.axis_index("dp")], recv).start()

    @pl.when(core != core_to)
    def _():
        piece(src, inbox, chip, core_to, send.at[0], recv).start()


def scatter(src, inbox, core_to, send, recv):
    chip, _ = split_dp()

    def one(k, carry):
        piece(src, inbox, (chip + k) % CHIPS, core_to, send.at[k], recv).start()
        return carry

    lax.fori_loop(1, CHIPS, one, 0)
    own_piece(src, inbox, core_to, send, recv)


def scatter_sent(src, inbox, core_to, send, recv):
    chip, core = split_dp()

    def one(k, carry):
        piece(src, inbox, chip, core_to, send.at[k], recv).wait_send()
        return carry

    lax.fori_loop(1, CHIPS, one, 0)

    @pl.when(core != core_to)
    def _():
        one(0, 0)


def arrived(whole, sem):
    pltpu.make_async_copy(whole, whole, sem).wait()


def sum_adapters(ids, inbox, rows, out, slot):
    def one(m, sums):
        term = inbox[m, rows].astype(jnp.float32)
        adapter = ids[m]
        return tuple(
            sums[a] + term * (adapter == a).astype(jnp.float32) for a in range(ADAPTERS)
        )

    zero = jnp.zeros((rows.stop - rows.start, HEAD), jnp.float32)
    sums = lax.fori_loop(0, MEMBERS, one, (zero,) * ADAPTERS)
    for a in range(ADAPTERS):
        out[slot, a] = sums[a].astype(jnp.bfloat16)


class Stream:
    def __init__(self, buf, out, owner, sems):
        self.buf, self.out, self.owner = buf, out, owner
        self.zs, self.zr, self.ys, self.yr, self.fs, self.fr, self.cs, self.cr, self.ks = sems
        self.half = buf.shape[1] // 2
        self.tensor = lax.axis_index("tensor")
        self.chip, self.core = split_dp()
        self.y, self.z = self.chip // N_Z, self.chip % N_Z

    def copy(self, slot, chip_to, core_to, send, recv, dst=None):
        return pltpu.make_async_remote_copy(
            src_ref=self.buf.at[slot],
            dst_ref=(self.buf if dst is None else dst).at[slot],
            send_sem=send,
            recv_sem=recv,
            device_id=(2 * chip_to + core_to, self.tensor),
            device_id_type=MESH,
        )

    def at(self, dy, dz):
        return ((self.y + dy + N_Y) % N_Y) * N_Z + (self.z + dz + N_Z) % N_Z

    def nearest_first(self):
        z, high = self.z, self.z // 2
        sources = (z + 1 - 2 * (z % 2), 2 - high, 3 * (1 - high))
        return [(z - source + N_Z) % N_Z for source in sources]

    def z_copy(self, d):
        return self.copy(
            self.chip, self.at(0, d), self.owner, self.zs.at[d - 1], self.zr.at[d - 1]
        )

    def y_copy(self, dz, dy):
        n = 3 * dz + dy - 1
        return self.copy(self.at(0, -dz), self.at(dy, 0), self.owner, self.ys.at[n], self.yr.at[n])

    def twin(self, n, slot):
        return self.copy(
            slot, self.chip, 1 - self.owner, self.cs.at[n], self.cr, self.out
        )

    def deliver(self, n, slot):
        self.twin(n, slot).start()
        pltpu.make_async_copy(self.buf.at[slot], self.out.at[slot], self.ks).start()

    def y_sends(self, dz, steps=(2, 1, 3)):
        for dy in steps:
            self.y_copy(dz, dy).start()
        self.deliver(dz, self.at(0, -dz))

    def forward(self, k, dz, side):
        part = pl.ds(0, self.half) if side == 0 else pl.ds(self.half, self.buf.shape[1] - self.half)
        slot, to = self.at(2 * side - 1, -dz), self.at(1 - 2 * side, 0)
        return self.forward_copy(k, slot, to, side, part)

    def forwarded(self, k, dz, side):
        part = pl.ds(0, self.half) if side == 0 else pl.ds(self.half, self.buf.shape[1] - self.half)
        return self.forward_copy(k, self.at(2, -dz), self.chip, side, part)

    def forward_copy(self, k, slot, to, side, part):
        return pltpu.make_async_remote_copy(
            src_ref=self.buf.at[slot, part],
            dst_ref=self.buf.at[slot, part],
            send_sem=self.fs.at[2 * k + side],
            recv_sem=self.fr.at[2 * k + side],
            device_id=(2 * to + self.owner, self.tensor),
            device_id_type=MESH,
        )

    def start(self):
        for d in (2, 1, 3):
            self.z_copy(d).start()
        self.y_sends(0, (1, 3))

    def pass_on(self, k, dz):
        for side, dy in enumerate((1, 3)):
            self.y_copy(dz, dy).wait_recv()
            self.forward(k, dz, side).start()
            self.deliver(4 + 3 * dz + dy - 1, self.at(-dy, -dz))

    def spread(self):
        near, middle, far = self.nearest_first()
        self.z_copy(near).wait_recv()
        self.y_sends(near, (1, 3))
        self.z_copy(middle).wait_recv()
        self.y_sends(middle)
        self.pass_on(0, 0)
        self.z_copy(far).wait_recv()
        self.y_sends(far)
        self.pass_on(1, near)

    def finish(self):
        near, middle, far = self.nearest_first()
        for dz in (middle, far):
            for dy in (1, 3, 2):
                self.y_copy(dz, dy).wait_recv()
                self.deliver(4 + 3 * dz + dy - 1, self.at(-dy, -dz))
            k, other = (0, 0) if dz is middle else (1, near)
            for side in range(2):
                self.forwarded(k, other, side).wait_recv()
            self.deliver(4 + 3 * other + 1, self.at(2, -other))

    def sent(self):
        near, middle, far = self.nearest_first()
        for d in range(1, N_Z):
            self.z_copy(d).wait_send()
        for dz, steps in ((0, (1, 3)), (near, (1, 3)), (middle, (1, 2, 3)), (far, (1, 2, 3))):
            for dy in steps:
                self.y_copy(dz, dy).wait_send()
        for k, dz in enumerate((0, near)):
            for side in range(2):
                self.forward(k, dz, side).wait_send()
        for n in range(CHIPS):
            self.twin(n, self.chip).wait_send()
        pltpu.make_async_copy(self.buf, self.out, self.ks).wait()

    def receive(self):
        arrived(self.out, self.cr)


STREAM_SEMS = [DMA((3,))] * 2 + [DMA((12,))] * 2 + [DMA((4,))] * 2 + [DMA((CHIPS,)), DMA, DMA]


def share(part, inbox, send, recv):
    dp, me = lax.axis_index("dp"), lax.axis_index("tensor")
    copies = []
    for n, other in enumerate(tensor_peers()):
        copies.append(
            pltpu.make_async_remote_copy(
                src_ref=part,
                dst_ref=inbox.at[me],
                send_sem=send.at[n],
                recv_sem=recv.at[n],
                device_id=(dp, other),
                device_id_type=MESH,
            )
        )
        copies[-1].start()
    inbox[me] = part[...]
    return copies


def fill_masks(seg, masks):
    u = lax.broadcasted_iota(jnp.int32, (BLOCK, BLOCK), 0)
    t = lax.broadcasted_iota(jnp.int32, (BLOCK, BLOCK), 1)
    docs = [
        jnp.broadcast_to(
            seg[:, b * BLOCK : (b + 1) * BLOCK].astype(jnp.float32), (BLOCK, BLOCK)
        )
        for b in range(BLOCKS)
    ]
    for i in range(BLOCKS):
        masks[i, BLOCK:] = jnp.where((docs[i].T == docs[i]) & (u <= t), 0.0, masked_score)
        if i:
            masks[i, :BLOCK] = jnp.where(docs[i - 1].T == docs[i], 0.0, masked_score)


ORDER = "A3 B3 A2 C3 B2 A1 C2 B1 A0 C1 B0 C0".split()


def attend(base, masks, low, up_half, keys, values, gs, dqs, plow, upout, mine, done):
    bf16, f32 = jnp.bfloat16, jnp.float32
    qcols = slice(0, HEADS * HEAD)
    kcols = slice(HEADS * HEAD, (HEADS + 1) * HEAD)
    vcols = slice((HEADS + 1) * HEAD, (HEADS + 2) * HEAD)
    scale = 1.0 / math.sqrt(HEAD)
    low_q, low_k, low_v = (
        jnp.concatenate([low[b, n * RANK : (n + 1) * RANK] for b in range(BLOCKS)], axis=1)
        for n in range(KINDS)
    )
    keys[...] = (base[:, kcols].astype(f32) + matmul(low_k, up_half[:, kcols], TN)).astype(bf16)
    values[...] = (base[:, vcols].astype(f32) + matmul(low_v, up_half[:, vcols], TN)).astype(bf16)
    up_q = up_half[:, qcols]
    held, grads, next_dk, next_dv = {}, {}, {}, {}
    own_k, own_v = {}, {}

    def window(i):
        return slice(max(i - 1, 0) * BLOCK, (i + 1) * BLOCK)

    def stage_a(i):
        rows = slice(i * BLOCK, (i + 1) * BLOCK)
        q_wide = base[rows, qcols].astype(f32) + matmul(low[i, 0:RANK], up_q, TN)
        q_wide = q_wide.astype(bf16)
        q = jnp.concatenate([q_wide[:, h * HEAD : (h + 1) * HEAD] for h in range(HEADS)], axis=0)
        held[i] = q, matmul(keys[window(i)], q, NT)

    def stage_b(i):
        q, scores = held.pop(i)
        mask = masks[i] if i else masks[0, BLOCK:]
        mask = jnp.concatenate([mask] * HEADS, axis=1)
        scores = scores * (scale * math.log2(math.e)) + mask
        top = jnp.max(scores, axis=0, keepdims=True)
        weights = jnp.exp2(scores - top)
        total = jnp.sum(weights, axis=0, keepdims=True)
        probs = weights * (1.0 / total)
        prob_grad = matmul(values[window(i)], gs[i], NT)
        row_dot = jnp.sum(probs * prob_grad, axis=0, keepdims=True)
        score_grad = (probs * (prob_grad - row_dot)).astype(bf16)
        grads[i] = q, probs.astype(bf16), score_grad

    def stage_c(i):
        q, probs, score_grad = grads.pop(i)
        dk = matmul(score_grad, q)
        dv = matmul(probs, gs[i])
        key = keys[window(i)]
        dq = (matmul(key.astype(f32).T.astype(bf16), score_grad) * scale).astype(bf16)
        dq = jnp.concatenate(
            [dq[:, h * BLOCK : (h + 1) * BLOCK] for h in range(HEADS)], axis=0
        )
        dqs[:, i * BLOCK : (i + 1) * BLOCK] = dq
        dk_own, dv_own = dk[-BLOCK:], dv[-BLOCK:]
        if i < BLOCKS - 1:
            dk_own, dv_own = dk_own + next_dk.pop(i), dv_own + next_dv.pop(i)
        if i:
            next_dk[i - 1], next_dv[i - 1] = dk[:BLOCK], dv[:BLOCK]
        own_k[i], own_v[i] = (dk_own * scale).astype(bf16), dv_own.astype(bf16)
        plow[i, 0:RANK] = matmul(up_q, dq).astype(bf16)
        plow[i, RANK : 2 * RANK] = matmul(up_half[:, kcols], own_k[i], NT).astype(bf16)
        plow[i, 2 * RANK :] = matmul(up_half[:, vcols], own_v[i], NT).astype(bf16)
        done(i)

    stages = {"A": stage_a, "B": stage_b, "C": stage_c}
    for item in ORDER:
        stages[item[0]](int(item[1]))

    gup = matmul(low_q, dqs[...], NT) * 0.5
    gup_k = sum(matmul(low[b, RANK : 2 * RANK], own_k[b]) for b in range(BLOCKS)) * 0.5
    gup_v = sum(matmul(low[b, 2 * RANK :], own_v[b]) for b in range(BLOCKS)) * 0.5
    for j in range(CHIPS):
        upout[j, 0:RANK] = gup[:, j * HEAD : (j + 1) * HEAD].astype(bf16)
        upout[j, RANK:] = ((gup_v if j % 2 else gup_k) * mine(j // 2)).astype(bf16)


def fused_kernel(
    ids_hbm, x_hbm, base_hbm, grad_hbm, seg_hbm, down_hbm, up_hbm, out_a, out_b, out_u,
    ids, x_ref, base, grad, seg, down_ref, up_ref, masks, loads,
    part, inbox, low, s1, r1, s2, r2,
    up_half, keys, values, gs, dqs, plow, up_part, shared, s3, r3,
    down_early, down_a, down_b, in_a, in_b, in_u, sa, sb, su, ra, rb, ru,
    buf_a, buf_b, buf_u, *sems,
):
    bf16, f32 = jnp.bfloat16, jnp.float32
    chip, core = split_dp()
    tensor, dp = lax.axis_index("tensor"), lax.axis_index("dp")
    fetch = [
        pltpu.make_async_copy(src, dst, loads.at[n])
        for n, (src, dst) in enumerate(
            [
                (ids_hbm, ids), (down_hbm, down_ref), (x_hbm.at[: 2 * BLOCK], x_ref.at[: 2 * BLOCK]), (up_hbm, up_ref),
                (grad_hbm, grad), (base_hbm, base), (seg_hbm, seg),
            ]
        )
    ]
    rest = pltpu.make_async_copy(x_hbm.at[2 * BLOCK :], x_ref.at[2 * BLOCK :], loads.at[7])
    for copy in fetch[:3] + [rest] + fetch[3:]:
        copy.start()

    barrier = pltpu.get_barrier_semaphore()
    greet_tensor(barrier)

    def greet(k, carry):
        other = (dp + k) % MEMBERS
        pl.semaphore_signal(barrier, inc=1, device_id=(other, tensor), device_id_type=MESH)
        return carry

    lax.fori_loop(1, MEMBERS, greet, 0)

    fetch[0].wait()
    adapter = ids[dp]
    fetch[1].wait()
    fetch[2].wait()
    for half in range(2):
        if half:
            rest.wait()
        rows = slice(2 * half * BLOCK, 2 * (half + 1) * BLOCK)
        partial_low = matmul(down_ref[adapter], x_ref[rows], NT)
        for b in range(2):
            part[2 * half + b] = partial_low[:, b * BLOCK : (b + 1) * BLOCK].astype(bf16)
    pl.semaphore_wait(barrier, N_TENSOR - 1 + MEMBERS - 1)
    copies = tensor_scatter(part, inbox, s1, r1)
    fetch[3].wait()
    up_half[...] = (up_ref[adapter].astype(f32) * 0.5).astype(bf16)
    fetch[6].wait()
    fill_masks(seg, masks)
    fetch[4].wait()
    for b in range(BLOCKS):
        for h in range(HEADS):
            tile = grad[b * BLOCK : (b + 1) * BLOCK, h * HEAD : (h + 1) * HEAD]
            gs[b, h * BLOCK : (h + 1) * BLOCK] = tile
    fetch[5].wait()
    received(copies)
    tensor_reduce(inbox, low)
    more = tensor_gather(low, s2, r2)
    received(more)
    copies = copies + more

    shares = {}

    def done(i):
        shares[i] = share(plow.at[i], shared.at[i], s3.at[i], r3.at[i])

    def mine(a):
        return (adapter == a).astype(f32)

    attend(base, masks, low, up_half, keys, values, gs, dqs, plow, up_part, mine, done)
    scatter(up_part, in_u, 1, su, ru)

    def low_grad(b):
        received(shares[b])
        total = shared[b, 0].astype(f32)
        for n in range(1, N_TENSOR):
            total = total + shared[b, n].astype(f32)
        return total.astype(bf16)

    early = jnp.concatenate([low_grad(b) for b in range(1, BLOCKS)], axis=1)
    wide = N_Z * HEAD
    for s in range(N_Y):
        cols = slice(s * wide, (s + 1) * wide)
        down_early[:, cols] = matmul(early, x_ref[BLOCK:, cols])
    late = low_grad(0)
    y, z = chip // N_Z, chip % N_Z
    for s, dy in enumerate((2, 1, 3, 0)):
        there = (y + dy) % N_Y
        cols = pl.ds(pl.multiple_of(there * wide, wide), wide)
        product = (matmul(late, x_ref[:BLOCK, cols]) + down_early[:, cols]).astype(bf16)
        for j in range(N_Z):
            tile = product[:, j * HEAD : (j + 1) * HEAD]
            down_a[there * N_Z + j] = tile[: 2 * RANK]
            down_b[there * N_Z + j] = tile[2 * RANK :]
        for j in range(N_Z):
            if dy:
                p = there * N_Z + (1 - z // 2) * (3 - j) + (z // 2) * j
            else:
                p = there * N_Z + (z + j) % N_Z
            n = (4 + 4 * s + j) if dy else j
            if dy or j:
                piece(down_a, in_a, p, 0, sa.at[n], ra).start()
                piece(down_b, in_b, p, 1, sb.at[n], rb).start()
    own_piece(down_a, in_a, 0, sa, ra)
    own_piece(down_b, in_b, 1, sb, rb)

    stream_a = Stream(buf_a, out_a, 0, sems[0:9])
    stream_b = Stream(buf_b, out_b, 1, sems[9:18])
    stream_u = Stream(buf_u, out_u, 1, sems[18:27])

    @pl.when(core == 0)
    def _():
        arrived(in_a, ra)
        sum_adapters(ids, in_a, slice(0, 2 * RANK), buf_a, chip)
        stream_a.start()
        stream_a.spread()
        stream_a.finish()
        stream_a.sent()
        stream_b.receive()
        stream_u.receive()

    @pl.when(core == 1)
    def _():
        arrived(in_u, ru)
        sum_adapters(ids, in_u, slice(0, RANK), buf_u, chip)

        def one(m, total):
            return total + in_u[m, RANK:].astype(f32)

        total = lax.fori_loop(0, MEMBERS, one, jnp.zeros((RANK, HEAD), f32))
        buf_u[chip, ADAPTERS] = total.astype(bf16)
        stream_u.start()
        arrived(in_b, rb)
        sum_adapters(ids, in_b, slice(0, RANK), buf_b, chip)
        stream_b.start()
        stream_u.spread()
        stream_b.spread()
        stream_u.finish()
        stream_b.finish()
        stream_u.sent()
        stream_b.sent()
        stream_a.receive()

    sent(copies + sum(shares.values(), []))
    scatter_sent(up_part, in_u, 1, su, ru)
    scatter_sent(down_a, in_a, 0, sa, ra)
    scatter_sent(down_b, in_b, 1, sb, rb)


def widen_kernel(a_ref, b_ref, u_ref, down_hbm, up_hbm, down, up, sems):
    stores = []
    for a in range(ADAPTERS):
        for j in range(CHIPS):
            cols = slice(j * HEAD, (j + 1) * HEAD)
            down[a, : 2 * RANK, cols] = a_ref[j, a].astype(jnp.float32)
            down[a, 2 * RANK :, cols] = b_ref[j, a].astype(jnp.float32)
            up[a, :, cols] = u_ref[j, a].astype(jnp.float32)
        for kind in range(2):
            cols = slice((CHIPS + kind) * HEAD, (CHIPS + kind + 1) * HEAD)
            up[a, :, cols] = u_ref[2 * a + kind, ADAPTERS].astype(jnp.float32)
        for n, (src, dst) in enumerate([(down, down_hbm), (up, up_hbm)]):
            stores.append(pltpu.make_async_copy(src.at[a], dst.at[a], sems.at[n, a]))
            stores[-1].start()
    for copy in stores:
        copy.wait()


def hbm():
    return pl.BlockSpec(memory_space=pl.ANY)


def per_device(x, base, grad, segments, ids, down, up):
    bf16, f32 = jnp.bfloat16, jnp.float32
    ids = ids.reshape(-1)
    x, base, grad, segments, ids, down, up = (
        pltpu.with_memory_space_constraint(v, pltpu.HBM)
        for v in (x, base, grad, segments, ids, down, up)
    )
    tokens, width = x.shape
    cols = base.shape[1]
    rows = KINDS * RANK
    limit = 40 * 1024 * 1024
    out_a, out_b, out_u = pl.pallas_call(
        fused_kernel,
        out_shape=(
            jax.ShapeDtypeStruct((CHIPS, ADAPTERS, 2 * RANK, HEAD), bf16),
            jax.ShapeDtypeStruct((CHIPS, ADAPTERS, RANK, HEAD), bf16),
            jax.ShapeDtypeStruct((CHIPS, ADAPTERS + 1, RANK, HEAD), bf16),
        ),
        in_specs=[hbm()] * 7,
        out_specs=(hbm(), hbm(), hbm()),
        scratch_shapes=[
            SMEM((MEMBERS,), jnp.int32),
            VMEM(x.shape, bf16), VMEM(base.shape, bf16), VMEM(grad.shape, bf16),
            VMEM(segments.shape, jnp.int32),
            VMEM(down.shape, bf16), VMEM(up.shape, bf16),
            VMEM((BLOCKS, 2 * BLOCK, BLOCK), f32), DMA((8,)),
            VMEM((BLOCKS, rows, BLOCK), bf16),
            VMEM((N_TENSOR, rows, BLOCK), bf16),
            VMEM((BLOCKS, rows, BLOCK), bf16),
            DMA((7,)), DMA((7,)), DMA((3,)), DMA((3,)),
            VMEM((RANK, cols), bf16),
            VMEM((tokens, HEAD), bf16),
            VMEM((tokens, HEAD), bf16),
            VMEM((BLOCKS, HEADS * BLOCK, HEAD), bf16),
            VMEM((HEADS * HEAD, tokens), bf16),
            VMEM((BLOCKS, rows, BLOCK), bf16),
            VMEM((CHIPS, 2 * RANK, HEAD), bf16),
            VMEM((BLOCKS, N_TENSOR, rows, BLOCK), bf16),
            DMA((BLOCKS, 7)), DMA((BLOCKS, 7)),
            VMEM((rows, width), f32),
            VMEM((CHIPS, 2 * RANK, HEAD), bf16),
            VMEM((CHIPS, RANK, HEAD), bf16),
            VMEM((MEMBERS, 2 * RANK, HEAD), bf16),
            VMEM((MEMBERS, RANK, HEAD), bf16),
            VMEM((MEMBERS, 2 * RANK, HEAD), bf16),
            DMA((CHIPS,)), DMA((CHIPS,)), DMA((CHIPS,)),
            DMA, DMA, DMA,
            VMEM((CHIPS, ADAPTERS, 2 * RANK, HEAD), bf16),
            VMEM((CHIPS, ADAPTERS, RANK, HEAD), bf16),
            VMEM((CHIPS, ADAPTERS + 1, RANK, HEAD), bf16),
        ] + STREAM_SEMS * 3,
        compiler_params=pltpu.CompilerParams(
            collective_id=0, has_side_effects=True, vmem_limit_bytes=limit
        ),
        name="fused",
    )(ids, x, base, grad, segments, down, up)

    return pl.pallas_call(
        widen_kernel,
        out_shape=(
            jax.ShapeDtypeStruct((ADAPTERS, rows, width), f32),
            jax.ShapeDtypeStruct((ADAPTERS, RANK, cols), f32),
        ),
        in_specs=[vmem()] * 3,
        out_specs=(hbm(), hbm()),
        scratch_shapes=[
            VMEM((ADAPTERS, rows, width), f32),
            VMEM((ADAPTERS, RANK, cols), f32),
            DMA((2, ADAPTERS)),
        ],
        compiler_params=pltpu.CompilerParams(vmem_limit_bytes=limit),
        name="widen",
    )(out_a, out_b, out_u)


def solution(mesh):
    placed = (
        P("dp", "tensor"),
        P("dp", "tensor"),
        P("dp", "tensor"),
        P("dp", None),
        P(),
        P(None, None, "tensor"),
        P(None, None, "tensor"),
    )
    return jax.shard_map(
        per_device,
        mesh=mesh,
        in_specs=placed,
        out_specs=(P(None, None, "tensor"), P(None, None, "tensor")),
        check_vma=False,
    )
```
